32 devices in a mesh: atoms: 16 (over z, x, core), dirs: 2 (over y).
Axes of the slice: x: 2, y: 2, z: 4, core: 2. Of those that a mesh axis runs over, the one named last changes fastest.
Arguments:
- queries: bfloat16 [32768, 128], P('atoms'), may hold values from -6 to 6
- keys: bfloat16 [32768, 128], P('atoms'), may hold values from -6 to 6
- values: bfloat16 [32768, 128], P('atoms'), may hold values from -6 to 6
- cotangent: bfloat16 [32768, 128], P('atoms'), may hold values from -6 to 6
- positions: float32 [3, 32768], P(None, 'atoms'), may hold values from -32 to 32
- species: int32 [32768], P('atoms'), may hold values from 0 to 4
- domain: int32 [32768], P('atoms'), may hold values from 0 to 16, as said below
- species_gain: float32 [5, 128], replicated, may hold values from 0.1 to 1.9
- frequency: float32 [32], replicated, may hold values from 0.02 to 1
- directions: float32 [3, 88], P(None, 'dirs'), may hold values from -1 to 1, as said below
- dir_weight: float32 [88], P('dirs'), may hold values from 0.003 to 0.03
- dir_mask: int32 [88], P('dirs'), may hold values from 0 to 1, as said below
Outputs:
- attended: bfloat16 [32768, 128], P(('atoms', 'dirs'))
- grad_queries: bfloat16 [32768, 128], P(('atoms', 'dirs'))
- grad_keys: bfloat16 [32768, 128], P(('atoms', 'dirs'))
- grad_values: bfloat16 [32768, 128], P(('atoms', 'dirs'))
The draws below stay inside these ranges and needn't reach their ends.
Inputs may be any that keep to these rules, and one draw needn't show every extreme that they name: The 2048 slots from b * 2048 on belong to domain b: they hold b for its atoms first, then 32768 // 2048 for empty slots; every domain has 1024 to 2048 atoms. `directions`: each column is a unit vector. `dir_mask`: exactly 86 entries are 1.
All inputs are finite; a program needn't handle non-finite values.
Results may differ from the reference program's by a relative error of at most 0.012.
Values may be sent and summed in bfloat16 or wider, within the bound.
No kernel may reach another device: no remote copies, remote signals or barrier semaphores. Data moves between devices by JAX's collectives and lax.ppermute only.
A program may use at most 128 MiB of HBM per device.

```python
import math
import jax
import jax.numpy as jnp
from jax import lax

F = 128
FREQS = 32
DIRS = 88
SPECIES = 5
ATOMS_DEV = 2048
ATOMS = 32768


def draw_domain(key, part):
    key = jax.random.fold_in(key, 7)
    domain_count = ATOMS // ATOMS_DEV
    count_key, pick_key = jax.random.split(key)
    filled = jax.random.randint(count_key, (domain_count,), ATOMS_DEV // 2, ATOMS_DEV + 1)
    picked = jax.random.permutation(pick_key, domain_count)
    filled = jnp.where(picked == 0, ATOMS_DEV, filled)
    filled = jnp.where(picked == 1, ATOMS_DEV // 2, filled)
    slot_index = jnp.arange(ATOMS, dtype=jnp.int32)
    owner = slot_index // ATOMS_DEV
    within = slot_index % ATOMS_DEV
    return jnp.where(within < filled[owner], owner, domain_count).astype(jnp.int32)


def draw_positions(key, part):
    key = jax.random.fold_in(key, 11)
    along_key, side_key = jax.random.split(key)
    domain_count = ATOMS // ATOMS_DEV
    owner = (jnp.arange(ATOMS, dtype=jnp.int32) // ATOMS_DEV).astype(jnp.float32)
    offset = jax.random.uniform(along_key, (ATOMS,), jnp.float32)
    along = (owner + offset) * 4.0 - 2.0 * domain_count
    across = jax.random.uniform(side_key, (2, ATOMS), jnp.float32, -16.0, 16.0)
    return jnp.concatenate([along[None, :], across], axis=0)


def draw_directions(key, part):
    key = jax.random.fold_in(key, 13)
    raw_vectors = jax.random.normal(key, (3, DIRS), jnp.float32)
    return raw_vectors / jnp.sqrt(jnp.sum(raw_vectors * raw_vectors, axis=0, keepdims=True) + 1e-06)


def draw_dir_mask(key, part):
    key = jax.random.fold_in(key, 17)
    ordering = jax.random.permutation(key, DIRS)
    return (ordering < DIRS - 2).astype(jnp.int32)


def place_ends(entries, stream_key, least, top_value):
    longest = entries.shape.index(max(entries.shape))
    spots = []
    for shift in (0, 1):
        where = [jax.random.randint(jax.random.fold_in(stream_key, axis), (), 0, length) for axis, length in enumerate(entries.shape)]
        where[longest] = (where[longest] + shift) % entries.shape[longest]
        spots.append(tuple(where))
    return entries.at[spots[0]].set(least).at[spots[1]].set(top_value)


def shard_levels(rng, dims, shards, smallest, largest):
    def one(axis_at, shards_of):
        draws = jax.random.uniform(jax.random.fold_in(jax.random.fold_in(rng, 6), axis_at), (shards_of,), jnp.float32, smallest / len(shards), largest / len(shards))
        return jnp.repeat(jnp.exp(draws), dims[axis_at] // shards_of).reshape((-1,) + (1,) * (len(dims) - axis_at - 1))

    factor_of = one(*shards[0])
    for cut in shards[1:]:
        factor_of = factor_of * one(*cut)
    return factor_of


def centred(own_key, extent, scale, bound, pieces=(), kind=jnp.bfloat16):
    entries = scale * jax.random.normal(own_key, extent, jnp.float32)
    if pieces:
        entries = entries * shard_levels(own_key, extent, pieces, -0.22, 0.18)
    return jnp.clip(entries, -bound, bound).astype(kind)


def setup_inputs(seed: int = 0) -> dict:
    seeds = jax.random.split(jax.random.key(seed), 13)
    queries = centred(seeds[0], (ATOMS, F), 1.0, 6.0, ((0, 16),))
    keys = centred(seeds[1], (ATOMS, F), 1.0, 6.0, ((0, 16),))
    values = centred(seeds[2], (ATOMS, F), 1.0, 6.0, ((0, 16),))
    cotangent = centred(seeds[3], (ATOMS, F), 1.0, 6.0, ((0, 16),))
    positions = draw_positions(jax.random.fold_in(seeds[12], 71), 0)
    species = place_ends(jax.random.randint(seeds[5], (ATOMS,), 0, SPECIES), jax.random.fold_in(seeds[5], 1), 0, SPECIES - 1).astype(jnp.int32)
    domain = draw_domain(jax.random.fold_in(seeds[12], 71), 0)
    species_gain = jnp.clip(1.0 + 0.18 * jax.random.normal(seeds[7], (SPECIES, F), jnp.float32), 0.1, 1.9)
    frequency = jnp.clip(jnp.exp(jax.random.uniform(seeds[8], (FREQS,), jnp.float32, math.log(0.02), math.log(1.0))), 0.02, 1.0)
    directions = draw_directions(jax.random.fold_in(seeds[12], 71), 0)
    dir_weight = jnp.clip(jnp.exp(math.log(0.03) - 2.3025851 * jax.random.uniform(seeds[10], (DIRS,), jnp.float32) ** shard_levels(seeds[10], (DIRS,), ((0, 2),), -0.2, 0.2)), 0.003, 0.03)
    dir_mask = draw_dir_mask(jax.random.fold_in(seeds[12], 71), 0)
    return dict(queries=queries, keys=keys, values=values, cotangent=cotangent, positions=positions, species=species, domain=domain, species_gain=species_gain, frequency=frequency, directions=directions, dir_weight=dir_weight, dir_mask=dir_mask)


def rotate(features, cosine, sine_val):
    half_width = features.shape[-1] // 2
    leading = features[..., :half_width]
    trailing = features[..., half_width:]
    return jnp.concatenate([leading * cosine - trailing * sine_val, leading * sine_val + trailing * cosine], axis=-1)

def rounded(matrix):
    return lax.optimization_barrier(matrix.astype(jnp.bfloat16)).astype(jnp.float32)

def reference(queries, keys, values, cotangent, positions, species, domain, species_gain, frequency, directions, dir_weight, dir_mask):
    slot_owner = (jnp.arange(ATOMS, dtype=jnp.int32) // ATOMS_DEV).astype(jnp.int32)
    alive_mask = (domain == slot_owner).astype(jnp.float32)[:, None]
    gain_rows = species_gain[species]
    keys_gained = keys.astype(jnp.float32) * gain_rows * alive_mask
    queries_full = queries.astype(jnp.float32)
    values_live = values.astype(jnp.float32) * alive_mask
    grad_live = cotangent.astype(jnp.float32) * alive_mask
    dir_coef = dir_weight * dir_mask.astype(jnp.float32) / math.sqrt(F * ATOMS_DEV)
    pair_freq = jnp.tile(frequency, F // 2 // FREQS)
    projected = directions[0][:, None] * positions[0][None, :] + directions[1][:, None] * positions[1][None, :]
    projected = projected + directions[2][:, None] * positions[2][None, :]
    highest = lax.Precision.HIGHEST

    def direction_step(totals, inputs_step):
        out_total, query_total, key_total, value_total = totals
        dir_proj, dir_scale = inputs_step
        phase_angle = dir_proj[:, None] * pair_freq[None, :]
        cosine = jnp.cos(phase_angle)
        sine_val = jnp.sin(phase_angle)
        query_rot = rounded(rotate(queries_full, cosine, sine_val))
        key_rot = rounded(rotate(keys_gained, cosine, sine_val))
        state_full = jnp.dot(key_rot.T, values_live, precision=highest, preferred_element_type=jnp.float32)
        state_b = rounded(state_full)
        out_total = out_total + dir_scale * jnp.dot(query_rot, state_b, precision=highest, preferred_element_type=jnp.float32)
        back_query = dir_scale * jnp.dot(grad_live, state_b.T, precision=highest, preferred_element_type=jnp.float32)
        query_total = query_total + rotate(back_query, cosine, -sine_val)
        state_grad = rounded(dir_scale * jnp.dot(query_rot.T, grad_live, precision=highest, preferred_element_type=jnp.float32))
        back_key = jnp.dot(values_live, state_grad.T, precision=highest, preferred_element_type=jnp.float32)
        key_total = key_total + rotate(back_key, cosine, -sine_val)
        value_total = value_total + jnp.dot(key_rot, state_grad, precision=highest, preferred_element_type=jnp.float32)
        return ((out_total, query_total, key_total, value_total), None)
    zeros_full = jnp.zeros((ATOMS, F), jnp.float32)
    totals, _ = lax.scan(direction_step, (zeros_full, zeros_full, zeros_full, zeros_full), (projected, dir_coef))
    out_total, query_total, key_total, value_total = totals
    attended = (out_total * alive_mask).astype(jnp.bfloat16)
    grad_queries = query_total.astype(jnp.bfloat16)
    grad_keys = (key_total * gain_rows * alive_mask).astype(jnp.bfloat16)
    grad_values = value_total.astype(jnp.bfloat16)
    return (attended, grad_queries, grad_keys, grad_values)
```

```python
import functools
import math

import jax
import jax.numpy as jnp
from jax import lax
from jax.experimental import pallas as pl
from jax.experimental.pallas import tpu as pltpu
from jax.sharding import PartitionSpec as P

BF16 = jnp.bfloat16
F32 = jnp.float32
GROUP = 4
LANES = 128
VMEM_LIMIT = 56 * 2**20

SIN_COEF = (4.4428679, -7.30744342, 3.59478808, -0.78437403)
COS_COEF = (1.41420408, -6.97764206, 5.71523839, -1.72834866)


def cos_sin_turns(turns):
    part = turns - jnp.round(turns)
    square = part * part
    sine = SIN_COEF[2] + square * SIN_COEF[3]
    sine = SIN_COEF[1] + square * sine
    sine = part * (SIN_COEF[0] + square * sine)
    cosine = COS_COEF[2] + square * COS_COEF[3]
    cosine = COS_COEF[1] + square * cosine
    cosine = COS_COEF[0] + square * cosine
    return 1.0 - sine * sine, sine * cosine


def states_kernel(
    chunk, dirs_ref, coef_ref, freq_ref, pos_ref, alive_ref, species_ref, gain_ref,
    q_ref, k_ref, v_ref, g_ref, state_ref, grad_ref, kt, qt, kr, qr,
):
    group = pl.program_id(0)
    atoms = pos_ref.shape[1]
    quarter = LANES // GROUP

    @pl.when(group == 0)
    def _():
        for start in range(0, atoms, chunk):
            cols = slice(start, start + chunk)
            alive = alive_ref[:, cols]
            species = species_ref[:, cols]
            gain = jnp.zeros((LANES, chunk), F32)
            for s in range(gain_ref.shape[1]):
                gain = jnp.where(species == s, gain_ref[:, s : s + 1], gain)
            kt[:, cols] = k_ref[cols, :].astype(F32).T * gain * alive
            qt[:, cols] = q_ref[cols, :].astype(F32).T * alive

    freq = freq_ref[...]
    for start in range(0, atoms, chunk):
        cols = slice(start, start + chunk)
        for i in range(GROUP):
            u = group * GROUP + i
            proj = (
                dirs_ref[0, u] * pos_ref[0:1, cols]
                + dirs_ref[1, u] * pos_ref[1:2, cols]
                + dirs_ref[2, u] * pos_ref[2:3, cols]
            )
            cosine, sine = cos_sin_turns(freq[:, :1] * proj)
            for src, dst in ((kt, kr), (qt, qr)):
                for m in range(2):
                    lead = src[quarter * m : quarter * (m + 1), cols]
                    trail = src[quarter * (m + 2) : quarter * (m + 3), cols]
                    row = (m - i) % GROUP * LANES + quarter * m
                    dst[row : row + quarter, cols] = (lead * cosine - trail * sine).astype(BF16)
                    row = (m + 2 - i) % GROUP * LANES + quarter * (m + 2)
                    dst[row : row + quarter, cols] = (lead * sine + trail * cosine).astype(BF16)

    for rot, other, out in ((kr, v_ref, state_ref), (qr, g_ref, grad_ref)):
        total = jnp.dot(rot[...], other[...], preferred_element_type=F32)
        for k in range(GROUP):
            for m in range(GROUP):
                rows = slice(k * LANES + m * quarter, k * LANES + (m + 1) * quarter)
                scale = coef_ref[group * GROUP + (m - k) % GROUP]
                out[rows, :] = (total[rows, :] * scale).astype(BF16)


def rolled_lanes(x, by):
    return x if by == 0 else pltpu.roll(x, by, axis=1)


def swapped(x):
    half = LANES // 2
    return jnp.concatenate([-x[:, half:], x[:, :half]], axis=1)


def rotate_kernel(wave_ref, pos_ref, q_ref, k_ref, qr_ref, kr_ref, cos_ref, sin_ref):
    position = pos_ref[...]
    wave = wave_ref[...]
    turns = (
        position[:, 0:1] * wave[0:1, :]
        + position[:, 1:2] * wave[1:2, :]
        + position[:, 2:3] * wave[2:3, :]
    )
    cosine, sine = cos_sin_turns(turns)
    cos_ref[...] = cosine.astype(BF16)
    sin_ref[...] = sine.astype(BF16)
    for src, dst in ((q_ref, qr_ref), (k_ref, kr_ref)):
        x = src[...]
        x_swapped = swapped(x)
        for k in range(GROUP):
            dst[:, k * LANES : (k + 1) * LANES] = (
                x * rolled_lanes(cosine, k * LANES // GROUP)
                + x_swapped * rolled_lanes(sine, k * LANES // GROUP)
            ).astype(BF16)


def mix_kernel(
    half_ref, state_ref, grad_ref, v_ref, g_ref, qr_ref, kr_ref, cos_ref, sin_ref,
    att_ref, gq_ref, gk_ref, gv_ref,
):
    del half_ref
    att_ref[...] = jnp.dot(qr_ref[...], state_ref[...], preferred_element_type=F32).astype(
        att_ref.dtype
    )
    gv_ref[...] = jnp.dot(kr_ref[...], grad_ref[...], preferred_element_type=F32).astype(
        gv_ref.dtype
    )
    rows = g_ref.shape[0]
    width = GROUP * LANES
    zero = jnp.zeros((rows, LANES), F32)
    sums = [zero, zero, zero, zero]
    for group in range(cos_ref.shape[1] // LANES):
        lanes = slice(group * LANES, (group + 1) * LANES)
        cosine = cos_ref[:, lanes].astype(F32)
        sine = sin_ref[:, lanes].astype(F32)
        cos_k = [rolled_lanes(cosine, k * LANES // GROUP) for k in range(GROUP)]
        sin_k = [rolled_lanes(sine, k * LANES // GROUP) for k in range(GROUP)]
        rows_g = slice(group * width, (group + 1) * width)
        for at, (left, right) in enumerate(((g_ref, state_ref), (v_ref, grad_ref))):
            back = lax.dot_general(
                left[...], right[rows_g, :], (((1,), (1,)), ((), ())), preferred_element_type=F32
            )
            for k in range(GROUP):
                part = back[:, k * LANES : (k + 1) * LANES]
                sums[2 * at] = sums[2 * at] + part * cos_k[k]
                sums[2 * at + 1] = sums[2 * at + 1] + part * sin_k[k]
    gq_ref[...] = (sums[0] - swapped(sums[1])).astype(gq_ref.dtype)
    gk_ref[...] = (sums[2] - swapped(sums[3])).astype(gk_ref.dtype)


def per_device(
    queries, keys, values, cotangent, positions, species, domain, species_gain, frequency,
    directions, dir_weight, dir_mask,
):
    atoms, feats = queries.shape
    dirs = dir_weight.shape[0]
    groups = dirs // GROUP
    rows = dirs * feats
    width = GROUP * feats
    alive = (domain == lax.axis_index("atoms")).astype(F32)
    turns_freq = frequency / (2.0 * math.pi)
    coef = dir_weight * dir_mask.astype(F32) / math.sqrt(feats * atoms)
    vmem = pl.BlockSpec(memory_space=pltpu.VMEM)
    smem = pl.BlockSpec(memory_space=pltpu.SMEM)
    params = functools.partial(pltpu.CompilerParams, vmem_limit_bytes=VMEM_LIMIT)

    states, grads = pl.pallas_call(
        functools.partial(states_kernel, 512),
        grid=(groups,),
        in_specs=[smem, smem] + [vmem] * 9,
        out_specs=[pl.BlockSpec((width, feats), lambda g: (g, 0))] * 2,
        out_shape=[jax.ShapeDtypeStruct((rows, feats), BF16)] * 2,
        scratch_shapes=[
            pltpu.VMEM((feats, atoms), F32),
            pltpu.VMEM((feats, atoms), F32),
            pltpu.VMEM((width, atoms), BF16),
            pltpu.VMEM((width, atoms), BF16),
        ],
        compiler_params=params(),
        cost_estimate=pl.CostEstimate(
            flops=4 * rows * atoms * feats, bytes_accessed=4 * rows * feats, transcendentals=0
        ),
        name="states",
    )(
        directions, coef, jnp.broadcast_to(turns_freq[:, None], (turns_freq.shape[0], LANES)),
        positions, alive[None, :], species[None, :], species_gain.T,
        queries, keys, values, cotangent,
    )

    both = jnp.concatenate([states, grads], axis=0)
    shard = lax.psum_scatter(both, "atoms", scatter_dimension=0, tiled=True)
    both = lax.all_gather(shard, "atoms", axis=0, tiled=True)

    species_ids = jnp.arange(species_gain.shape[0], dtype=jnp.int32)
    chosen = (species[:, None] == species_ids[None, :]).astype(F32)
    gain_rows = jnp.sum(chosen[:, :, None] * species_gain[None, :, :], axis=1) * alive[:, None]
    wave = (directions[:, :, None] * turns_freq[None, None, :]).reshape(3, groups * LANES)
    tile = 512
    by_group = pl.BlockSpec((tile, width), lambda n, g: (n, g))
    by_rows = pl.BlockSpec((tile, feats), lambda n, g: (n, 0))
    lanes_g = pl.BlockSpec((tile, LANES), lambda n, g: (n, g))
    q_rot, k_rot, cosines, sines = pl.pallas_call(
        rotate_kernel,
        grid=(atoms // tile, groups),
        in_specs=[
            pl.BlockSpec((3, LANES), lambda n, g: (0, g)),
            pl.BlockSpec((tile, 3), lambda n, g: (n, 0)),
            by_rows,
            by_rows,
        ],
        out_specs=[by_group, by_group, lanes_g, lanes_g],
        out_shape=[
            jax.ShapeDtypeStruct((atoms, rows), BF16),
            jax.ShapeDtypeStruct((atoms, rows), BF16),
            jax.ShapeDtypeStruct((atoms, groups * LANES), BF16),
            jax.ShapeDtypeStruct((atoms, groups * LANES), BF16),
        ],
        compiler_params=params(),
        cost_estimate=pl.CostEstimate(
            flops=atoms * rows * 10, bytes_accessed=5 * atoms * rows, transcendentals=0
        ),
        name="rotations",
    )(wave, positions.T, queries.astype(F32), keys.astype(F32) * gain_rows)

    states, grads = both[:rows], both[rows:]
    half_rows = atoms // 2
    block = 256
    steps = half_rows // block
    mine = lax.axis_index("dirs")

    def mix(half, dtype):
        def spec(lanes):
            return pl.BlockSpec((block, lanes), lambda n, half: (half[0] * steps + n, 0))

        out = pl.BlockSpec((block, feats), lambda n, half: (n, 0))
        whole = pl.BlockSpec((rows, feats), lambda n, half: (0, 0), pipeline_mode=pl.Buffered(1))
        return pl.pallas_call(
            mix_kernel,
            grid_spec=pltpu.PrefetchScalarGridSpec(
                num_scalar_prefetch=1,
                grid=(steps,),
                in_specs=[
                    whole, whole, spec(feats), spec(feats), spec(rows), spec(rows),
                    spec(groups * LANES), spec(groups * LANES),
                ],
                out_specs=[out] * 4,
            ),
            out_shape=[jax.ShapeDtypeStruct((half_rows, feats), dtype)] * 4,
            compiler_params=params(),
            cost_estimate=pl.CostEstimate(
                flops=8 * rows * half_rows * feats, bytes_accessed=5 * half_rows * rows,
                transcendentals=0,
            ),
            name="mix",
        )(
            half[None].astype(jnp.int32), states, grads, values, cotangent, q_rot, k_rot,
            cosines, sines,
        )

    away = jnp.concatenate(mix(1 - mine, BF16), axis=1)
    arrived = lax.ppermute(away, "dirs", [(0, 1), (1, 0)])
    kept = mix(mine, F32)
    alive_own = lax.dynamic_slice(alive, (mine * half_rows,), (half_rows,))[:, None]
    gain_own = lax.dynamic_slice(gain_rows, (mine * half_rows, 0), (half_rows, feats))
    results = []
    for at, scale in enumerate((alive_own, alive_own, gain_own, alive_own)):
        other = arrived[:, at * feats : (at + 1) * feats].astype(F32)
        results.append(((kept[at] + other) * scale).astype(BF16))
    return tuple(results)


def solution(mesh):
    return jax.shard_map(
        per_device,
        mesh=mesh,
        in_specs=(
            P("atoms", None),
            P("atoms", None),
            P("atoms", None),
            P("atoms", None),
            P(None, "atoms"),
            P("atoms"),
            P("atoms"),
            P(),
            P(),
            P(None, "dirs"),
            P("dirs"),
            P("dirs"),
        ),
        out_specs=(
            P(("atoms", "dirs"), None),
            P(("atoms", "dirs"), None),
            P(("atoms", "dirs"), None),
            P(("atoms", "dirs"), None),
        ),
        check_vma=False,
    )
```

```python
import functools
import math

import jax
import jax.numpy as jnp
from jax import lax
from jax.experimental import pallas as pl
from jax.experimental.pallas import tpu as pltpu
from jax.sharding import PartitionSpec as P

BF16 = jnp.bfloat16
F32 = jnp.float32
GROUP = 4
QUADS = 4
LANES = 128
QUARTER = LANES // QUADS
WIDTH = GROUP * LANES
VMEM_LIMIT = 56 * 2**20
CHUNKS = (3, 3, 3, 2)

SIN_COEF = (4.4428679, -7.30744342, 3.59478808, -0.78437403)
COS_COEF = (1.41420408, -6.97764206, 5.71523839, -1.72834866)


def cos_sin_turns(turns):
    part = turns - jnp.round(turns)
    square = part * part
    sine = SIN_COEF[2] + square * SIN_COEF[3]
    sine = SIN_COEF[1] + square * sine
    sine = part * (SIN_COEF[0] + square * sine)
    cosine = COS_COEF[2] + square * COS_COEF[3]
    cosine = COS_COEF[1] + square * cosine
    cosine = COS_COEF[0] + square * cosine
    return 1.0 - sine * sine, sine * cosine


def column(row):
    size = row.shape[1]
    at_row = lax.broadcasted_iota(jnp.int32, (size, size), 0)
    at_lane = lax.broadcasted_iota(jnp.int32, (size, size), 1)
    return jnp.sum(jnp.where(at_row == at_lane, row, 0.0), axis=1, keepdims=True)


def place_of(index):
    return index & 1, (index >> 1) & 1, (index >> 2) & 3


def prepare_kernel(
    index_ref, domain_ref, species_ref, gain_ref, q_ref, k_ref, v_ref, g_ref,
    qt_ref, kt_ref, vt_ref, gt_ref, gain_out,
):
    alive = (domain_ref[...] == index_ref[0]).astype(F32)
    species = species_ref[...]
    gain = jnp.zeros(gain_out.shape, F32)
    for s in range(gain_ref.shape[0]):
        gain = jnp.where(species == s, column(gain_ref[s : s + 1, :]), gain)
    gain_out[...] = gain
    kt_ref[...] = k_ref[...].astype(F32).T * gain * alive
    qt_ref[...] = q_ref[...].astype(F32).T * alive
    vt_ref[...] = (v_ref[...].astype(F32).T * alive).astype(BF16)
    gt_ref[...] = (g_ref[...].astype(F32).T * alive).astype(BF16)


def states_kernel(
    first, chunk, part, scale, index_ref, dirs_ref, weight_ref, mask_ref, freq_ref, pos_ref,
    qt_ref, kt_ref, v_ref, g_ref, kk_ref, ks_ref, sk_ref, ss_ref, kr_ref, qr_ref, cos_ref,
    sin_ref, k_total, q_total, slots,
):
    group = first + pl.program_id(0)
    atoms = pos_ref.shape[1]
    core, pair, quad = place_of(index_ref[0])
    freq = column(freq_ref[...]) * (1.0 / (2.0 * math.pi))
    for start in range(0, atoms, chunk):
        for at in range(start, start + chunk, part):
            cols = slice(at, at + part)
            for i in range(GROUP):
                u = group * GROUP + i
                proj = (
                    dirs_ref[0, u] * pos_ref[0:1, cols]
                    + dirs_ref[1, u] * pos_ref[1:2, cols]
                    + dirs_ref[2, u] * pos_ref[2:3, cols]
                )
                cosine, sine = cos_sin_turns(freq * proj)
                cos_ref[i * QUARTER : (i + 1) * QUARTER, cols] = cosine.astype(BF16)
                sin_ref[i * QUARTER : (i + 1) * QUARTER, cols] = sine.astype(BF16)
                for src, dst in ((kt_ref, kr_ref), (qt_ref, qr_ref)):
                    for m in range(2):
                        lead = src[QUARTER * m : QUARTER * (m + 1), cols]
                        trail = src[QUARTER * (m + 2) : QUARTER * (m + 3), cols]
                        row = i * LANES + QUARTER * m
                        dst[row : row + QUARTER, cols] = (lead * cosine - trail * sine).astype(BF16)
                        row = row + 2 * QUARTER
                        dst[row : row + QUARTER, cols] = (lead * sine + trail * cosine).astype(BF16)
        cols = slice(start, start + chunk)
        for rot, other, total in ((kr_ref, v_ref, k_total), (qr_ref, g_ref, q_total)):
            term = jnp.dot(rot[:, cols], other[cols, :], preferred_element_type=F32)
            total[...] = term if start == 0 else total[...] + term

    for kind, total in ((0, k_total), (1, q_total)):
        for i in range(GROUP):
            u = group * GROUP + i
            coef = weight_ref[u] * mask_ref[u].astype(F32) * scale
            rows = slice(i % 2 * QUARTER, (i % 2 + 1) * QUARTER)
            for m in range(QUADS):
                row = i * LANES + m * QUARTER
                slots[kind ^ core, (i // 2) ^ pair, (m - quad) & 3, rows, :] = (
                    total[row : row + QUARTER, :] * coef
                ).astype(BF16)
    for a, b, out in ((0, 0, kk_ref), (0, 1, ks_ref), (1, 0, sk_ref), (1, 1, ss_ref)):
        out[...] = slots[a, b]


def mix_kernel(
    has_totals, final, part, index_ref, half_ref, *refs,
):
    del half_ref
    refs = list(refs)
    sources, refs = refs[:4], refs[4:]
    vt_ref, gt_ref, kr_ref, qr_ref, cos_ref, sin_ref = refs[:6]
    refs = refs[6:]
    if final:
        gain_ref, refs = refs[0], refs[1:]
    if has_totals:
        before, refs = refs[:4], refs[4:]
    outs, refs = refs[:4], refs[4:]
    slots, states, states_t = refs[:3]
    totals = refs[3:7] if final else outs
    group = pl.program_id(1)
    groups = pl.num_programs(1)
    core, pair, quad = place_of(index_ref[0])

    @pl.when((group == 0) & (pl.program_id(0) == 0))
    def _():
        for at, source in enumerate(sources):
            slots[at // 2, at % 2] = source[...].reshape(slots.shape[2:])
        for g in range(slots.shape[3] // (2 * QUARTER)):
            for kind in range(2):
                for i in range(GROUP):
                    start = g * 2 * QUARTER + i % 2 * QUARTER
                    for m in range(QUADS):
                        states[kind, g, i * LANES + m * QUARTER : i * LANES + (m + 1) * QUARTER, :] = slots[
                            kind ^ core, (i // 2) ^ pair, (m - quad) & 3, start : start + QUARTER, :
                        ]
                    whole = states[kind, g, i * LANES : (i + 1) * LANES, :]
                    states_t[kind, g, :, i * LANES : (i + 1) * LANES] = (
                        whole.astype(F32).T.astype(BF16)
                    )

    @pl.when(group == 0)
    def _():
        for at, total in enumerate(totals):
            total[...] = before[at][...] if has_totals else jnp.zeros_like(total)

    for start in range(0, vt_ref.shape[1], part):
        cols = slice(start, start + part)
        for kind, rot, direct in ((0, qr_ref, totals[0]), (1, kr_ref, totals[3])):
            direct[:, cols] += jnp.dot(
                states_t[kind, group], rot[:, cols], preferred_element_type=F32
            )
        for kind, fixed, turned in ((0, gt_ref, totals[1]), (1, vt_ref, totals[2])):
            back = jnp.dot(states[kind, group], fixed[:, cols], preferred_element_type=F32)
            for m in range(2):
                lead_rows = slice(QUARTER * m, QUARTER * (m + 1))
                trail_rows = slice(QUARTER * (m + 2), QUARTER * (m + 3))
                lead_total = turned[lead_rows, cols]
                trail_total = turned[trail_rows, cols]
                for i in range(GROUP):
                    cosine = cos_ref[i * QUARTER : (i + 1) * QUARTER, cols].astype(F32)
                    sine = sin_ref[i * QUARTER : (i + 1) * QUARTER, cols].astype(F32)
                    row = i * LANES + QUARTER * m
                    lead = back[row : row + QUARTER, :]
                    trail = back[row + 2 * QUARTER : row + 3 * QUARTER, :]
                    lead_total = lead_total + (lead * cosine + trail * sine)
                    trail_total = trail_total + (trail * cosine - lead * sine)
                turned[lead_rows, cols] = lead_total
                turned[trail_rows, cols] = trail_total

    if final:
        @pl.when(group == groups - 1)
        def _():
            for at, (total, out) in enumerate(zip(totals, outs)):
                whole = total[...] * gain_ref[...] if at == 2 else total[...]
                out[...] = whole.T.astype(out.dtype)


def added(*terms):
    return sum(term.astype(F32) for term in terms).astype(BF16)


def per_device(
    atom_devices, queries, keys, values, cotangent, positions, species, domain, species_gain,
    frequency, directions, dir_weight, dir_mask,
):
    atoms, feats = queries.shape
    index = lax.axis_index("atoms")[None].astype(jnp.int32)
    mine = lax.axis_index("dirs").astype(jnp.int32)
    vmem = pl.BlockSpec(memory_space=pltpu.VMEM)
    smem = pl.BlockSpec(memory_space=pltpu.SMEM)
    params = pltpu.CompilerParams(vmem_limit_bytes=VMEM_LIMIT)
    shape = jax.ShapeDtypeStruct

    qt, kt, vt, gt, gain = pl.pallas_call(
        prepare_kernel,
        in_specs=[smem] + [vmem] * 7,
        out_specs=[vmem] * 5,
        out_shape=[
            shape((feats, atoms), F32), shape((feats, atoms), F32), shape((feats, atoms), BF16),
            shape((feats, atoms), BF16), shape((feats, atoms), F32),
        ],
        compiler_params=params,
        name="prepare",
    )(index, domain[None, :], species[None, :], species_gain, queries, keys, values, cotangent)

    chunk = min(512, atoms)
    part = min(256, chunk)

    def make_states(first, groups):
        sent = (QUADS, groups * 2 * QUARTER, feats)
        sent_spec = pl.BlockSpec((QUADS, 2 * QUARTER, feats), lambda g: (0, g, 0))
        results = pl.pallas_call(
            functools.partial(states_kernel, first, chunk, part, 1.0 / math.sqrt(feats * atoms)),
            grid=(groups,),
            in_specs=[smem] * 4 + [vmem] * 6,
            out_specs=[sent_spec] * 4
            + [pl.BlockSpec((WIDTH, atoms), lambda g: (g, 0))] * 2
            + [pl.BlockSpec((GROUP * QUARTER, atoms), lambda g: (g, 0))] * 2,
            out_shape=[shape(sent, BF16)] * 4
            + [shape((groups * WIDTH, atoms), BF16)] * 2
            + [shape((groups * GROUP * QUARTER, atoms), BF16)] * 2,
            scratch_shapes=[
                pltpu.VMEM((WIDTH, feats), F32),
                pltpu.VMEM((WIDTH, feats), F32),
                pltpu.VMEM((2, 2, QUADS, 2 * QUARTER, feats), BF16),
            ],
            compiler_params=params,
            cost_estimate=pl.CostEstimate(
                flops=8 * groups * WIDTH * atoms * feats,
                bytes_accessed=6 * groups * WIDTH * atoms, transcendentals=0,
            ),
            name="states",
        )(
            index, directions, dir_weight, dir_mask, frequency[None, :], positions, qt, kt,
            values, cotangent,
        )
        return results[:4], results[4:]

    def moved(x, target):
        return lax.ppermute(x, "atoms", [(i, target(i)) for i in range(atom_devices)])

    def by_core(x):
        return moved(x, lambda i: i ^ 1)

    def by_pair(x):
        return moved(x, lambda i: i ^ 2)

    def by_quad(x, step):
        return moved(x, lambda i: (i & ~12) | ((((i >> 2) + step) & 3) << 2))

    def summed(pieces):
        kept_kept, kept_sent, sent_kept, sent_sent = pieces
        arrived = by_core(sent_sent)
        arrived_kept = by_core(sent_kept)
        crossed = by_pair(added(kept_sent, arrived))
        half = added(kept_kept, arrived_kept, crossed)
        quarter = added(half[0], *(by_quad(half[step], step) for step in range(1, QUADS)))
        whole = quarter
        for step in range(16, atom_devices, 16):
            whole = added(whole, moved(quarter, lambda i: (i + step) % atom_devices))
        gathered = [whole] + [by_quad(whole, QUADS - step) for step in range(1, QUADS)]
        half = jnp.concatenate(gathered, axis=0)
        other = by_pair(half)
        return half, other, by_core(half), by_core(other)

    half_atoms = atoms // 2

    def mix(half, pieces, groups, kept, totals, final, dtype):
        blocks = 1 if final else 2
        mix_part = min(256, half_atoms)

        def at(n, half):
            return half[0] + n

        cols = lambda n, g, index, half: (0, at(n, half))
        rotated = lambda n, g, index, half: (g, at(n, half))
        rows_all = pl.BlockSpec((feats, half_atoms), cols)
        operands = [*pieces, vt, gt, *kept]
        specs = (
            [vmem] * 4
            + [rows_all] * 2
            + [pl.BlockSpec((WIDTH, half_atoms), rotated)] * 2
            + [pl.BlockSpec((GROUP * QUARTER, half_atoms), rotated)] * 2
        )
        if final:
            operands.append(gain)
            specs.append(rows_all)
        if totals is not None:
            operands += totals
            specs += [rows_all] * 4
        scratch = [
            pltpu.VMEM((2, 2, QUADS, groups * 2 * QUARTER, feats), BF16),
            pltpu.VMEM((2, groups, WIDTH, feats), BF16),
            pltpu.VMEM((2, groups, feats, WIDTH), BF16),
        ]
        if final:
            out_specs = [pl.BlockSpec((half_atoms, feats), lambda n, g, index, half: (0, 0))] * 4
            out_shape = [shape((half_atoms, feats), dtype)] * 4
            scratch += [pltpu.VMEM((feats, half_atoms), F32)] * 4
        else:
            out_specs = [rows_all] * 4
            out_shape = [shape((feats, atoms), F32)] * 4
        return pl.pallas_call(
            functools.partial(mix_kernel, totals is not None, final, mix_part),
            grid_spec=pltpu.PrefetchScalarGridSpec(
                num_scalar_prefetch=2,
                grid=(blocks, groups),
                in_specs=specs,
                out_specs=out_specs,
                scratch_shapes=scratch,
            ),
            out_shape=out_shape,
            compiler_params=params,
            cost_estimate=pl.CostEstimate(
                flops=8 * groups * WIDTH * blocks * half_atoms * feats,
                bytes_accessed=5 * groups * WIDTH * blocks * half_atoms, transcendentals=0,
            ),
            name="mix",
        )(index, half[None], *operands)

    made = []
    first = 0
    for groups in CHUNKS:
        pieces, kept = make_states(first, groups)
        made.append((summed(pieces), kept, groups))
        first += groups
    totals = None
    for pieces, kept, groups in made[:-1]:
        totals = mix(jnp.int32(0), pieces, groups, kept, totals, False, F32)
    pieces, kept, groups = made[-1]
    away = mix(1 - mine, pieces, groups, kept, totals, True, BF16)
    arrived = [lax.ppermute(x, "dirs", [(0, 1), (1, 0)]) for x in away]
    own = mix(mine, pieces, groups, kept, totals, True, F32)
    return tuple(
        (ours + theirs.astype(F32)).astype(BF16) for ours, theirs in zip(own, arrived)
    )


def solution(mesh):
    return jax.shard_map(
        functools.partial(per_device, mesh.shape["atoms"]),
        mesh=mesh,
        in_specs=(
            P("atoms", None),
            P("atoms", None),
            P("atoms", None),
            P("atoms", None),
            P(None, "atoms"),
            P("atoms"),
            P("atoms"),
            P(),
            P(),
            P(None, "dirs"),
            P("dirs"),
            P("dirs"),
        ),
        out_specs=(
            P(("atoms", "dirs"), None),
            P(("atoms", "dirs"), None),
            P(("atoms", "dirs"), None),
            P(("atoms", "dirs"), None),
        ),
        check_vma=False,
    )
```

```python
import functools
import math

import jax
import jax.numpy as jnp
from jax import lax
from jax.experimental import pallas as pl
from jax.experimental.pallas import tpu as pltpu
from jax.sharding import PartitionSpec as P

BF16 = jnp.bfloat16
F32 = jnp.float32
GROUP = 4
QUADS = 4
LANES = 128
QUARTER = LANES // QUADS
WIDTH = GROUP * LANES
VMEM_LIMIT = 30 * 2**20
CHUNKS = (4, 4, 3)

SIN_COEF = (4.4428679, -7.30744342, 3.59478808, -0.78437403)
COS_COEF = (1.41420408, -6.97764206, 5.71523839, -1.72834866)


def cos_sin_turns(turns):
    part = turns - jnp.round(turns)
    square = part * part
    sine = SIN_COEF[2] + square * SIN_COEF[3]
    sine = SIN_COEF[1] + square * sine
    sine = part * (SIN_COEF[0] + square * sine)
    cosine = COS_COEF[2] + square * COS_COEF[3]
    cosine = COS_COEF[1] + square * cosine
    cosine = COS_COEF[0] + square * cosine
    return 1.0 - sine * sine, sine * cosine


def column(row):
    size = row.shape[1]
    at_row = lax.broadcasted_iota(jnp.int32, (size, size), 0)
    at_lane = lax.broadcasted_iota(jnp.int32, (size, size), 1)
    return jnp.sum(jnp.where(at_row == at_lane, row, 0.0), axis=1, keepdims=True)


def place_of(index):
    return index & 1, (index >> 1) & 1, (index >> 2) & 3


def prepare_kernel(
    index_ref, domain_ref, species_ref, gain_ref, q_ref, k_ref, v_ref, g_ref,
    qt_ref, kt_ref, vt_ref, gt_ref, gain_out,
):
    alive = (domain_ref[...] == index_ref[0]).astype(F32)
    species = species_ref[...]
    gain = jnp.zeros(gain_out.shape, F32)
    for s in range(gain_ref.shape[0]):
        gain = jnp.where(species == s, column(gain_ref[s : s + 1, :]), gain)
    gain_out[...] = gain
    kt_ref[...] = k_ref[...].astype(F32).T * gain * alive
    qt_ref[...] = (q_ref[...].astype(F32).T * alive).astype(BF16)
    vt_ref[...] = (v_ref[...].astype(F32).T * alive).astype(BF16)
    gt_ref[...] = (g_ref[...].astype(F32).T * alive).astype(BF16)


def states_kernel(
    first, part, scale, index_ref, dirs_ref, weight_ref, mask_ref, freq_ref, pos_ref,
    qt_ref, kt_ref, v_ref, g_ref, *refs,
):
    kept_ref, sent_ref, cos_ref, sin_ref, kr, qr, slots = refs[-7:]
    group = first + pl.program_id(0)
    atoms = pos_ref.shape[1]
    core, pair, quad = place_of(index_ref[0])
    freq = column(freq_ref[...]) * (1.0 / (2.0 * math.pi))
    for start in range(0, atoms, part):
        cols = slice(start, start + part)
        for i in range(GROUP):
            u = group * GROUP + i
            proj = (
                dirs_ref[0, u] * pos_ref[0:1, cols]
                + dirs_ref[1, u] * pos_ref[1:2, cols]
                + dirs_ref[2, u] * pos_ref[2:3, cols]
            )
            cosine, sine = cos_sin_turns(freq * proj)
            cos_ref[i * QUARTER : (i + 1) * QUARTER, cols] = cosine.astype(BF16)
            sin_ref[i * QUARTER : (i + 1) * QUARTER, cols] = sine.astype(BF16)
            for src, dst in ((kt_ref, kr), (qt_ref, qr)):
                for m in range(2):
                    lead = src[QUARTER * m : QUARTER * (m + 1), cols].astype(F32)
                    trail = src[QUARTER * (m + 2) : QUARTER * (m + 3), cols].astype(F32)
                    row = i * LANES + QUARTER * m
                    dst[row : row + QUARTER, cols] = (lead * cosine - trail * sine).astype(BF16)
                    row = row + 2 * QUARTER
                    dst[row : row + QUARTER, cols] = (lead * sine + trail * cosine).astype(BF16)

    for kind, rot, other in ((0, kr, v_ref), (1, qr, g_ref)):
        total = jnp.dot(rot[...], other[...], preferred_element_type=F32)
        for i in range(GROUP):
            u = group * GROUP + i
            coef = weight_ref[u] * mask_ref[u].astype(F32) * scale
            rows = slice(i % 2 * QUARTER, (i % 2 + 1) * QUARTER)
            for m in range(QUADS):
                row = i * LANES + m * QUARTER
                slots[kind ^ core, (i // 2) ^ pair, (m - quad) & 3, rows, :] = (
                    total[row : row + QUARTER, :] * coef
                ).astype(BF16)
    kept_ref[...] = slots[0]
    sent_ref[...] = slots[1]


def rotated(x, cosine, sine):
    pieces = []
    for i in range(GROUP):
        c = cosine[i * QUARTER : (i + 1) * QUARTER]
        s = sine[i * QUARTER : (i + 1) * QUARTER]
        quarters = [x[m * QUARTER : (m + 1) * QUARTER] for m in range(QUADS)]
        pieces += [quarters[m] * c - quarters[m + 2] * s for m in range(2)]
        pieces += [quarters[m] * s + quarters[m + 2] * c for m in range(2)]
    return jnp.concatenate(pieces, axis=0)


def mix_kernel(
    has_totals, final, part, index_ref, half_ref, *refs,
):
    del half_ref
    refs = list(refs)
    sources, refs = refs[:4], refs[4:]
    vt_ref, gt_ref, kt_ref, qt_ref, cos_ref, sin_ref = refs[:6]
    refs = refs[6:]
    if final:
        gain_ref, refs = refs[0], refs[1:]
    if has_totals:
        before, refs = refs[:4], refs[4:]
    out_count = 1 if final else 4
    outs, refs = refs[:out_count], refs[out_count:]
    slots, states, states_t = refs[:3]
    totals = refs[3:7]
    group = pl.program_id(1)
    groups = pl.num_programs(1)
    core, pair, quad = place_of(index_ref[0])

    @pl.when((group == 0) & (pl.program_id(0) == 0))
    def _():
        for at, source in enumerate(sources):
            slots[at // 2, at % 2] = source[...].reshape(slots.shape[2:])
        for g in range(slots.shape[3] // (2 * QUARTER)):
            for kind in range(2):
                for i in range(GROUP):
                    start = g * 2 * QUARTER + i % 2 * QUARTER
                    for m in range(QUADS):
                        row = i * LANES + m * QUARTER
                        states[kind, g, row : row + QUARTER, :] = slots[
                            kind ^ core, (i // 2) ^ pair, (m - quad) & 3,
                            start : start + QUARTER, :,
                        ]
                    whole = states[kind, g, i * LANES : (i + 1) * LANES, :]
                    states_t[kind, g, :, i * LANES : (i + 1) * LANES] = (
                        whole.astype(F32).T.astype(BF16)
                    )

    @pl.when(group == 0)
    def _():
        for at, total in enumerate(totals):
            total[...] = before[at][...].astype(F32) if has_totals else jnp.zeros_like(total)

    for start in range(0, vt_ref.shape[1], part):
        cols = slice(start, start + part)
        cosine = cos_ref[:, cols]
        sine = sin_ref[:, cols]
        for kind, x_ref, direct in ((0, qt_ref, totals[0]), (1, kt_ref, totals[3])):
            turned = rotated(x_ref[:, cols].astype(BF16), cosine, sine)
            direct[:, cols] += jnp.dot(states_t[kind, group], turned, preferred_element_type=F32)
        cosine = cosine.astype(F32)
        sine = sine.astype(F32)
        for kind, fixed, turned in ((0, gt_ref, totals[1]), (1, vt_ref, totals[2])):
            back = jnp.dot(states[kind, group], fixed[:, cols], preferred_element_type=F32)
            for m in range(2):
                lead_rows = slice(QUARTER * m, QUARTER * (m + 1))
                trail_rows = slice(QUARTER * (m + 2), QUARTER * (m + 3))
                lead_total = turned[lead_rows, cols]
                trail_total = turned[trail_rows, cols]
                for i in range(GROUP):
                    c = cosine[i * QUARTER : (i + 1) * QUARTER]
                    s = sine[i * QUARTER : (i + 1) * QUARTER]
                    row = i * LANES + QUARTER * m
                    lead = back[row : row + QUARTER, :]
                    trail = back[row + 2 * QUARTER : row + 3 * QUARTER, :]
                    lead_total = lead_total + (lead * c + trail * s)
                    trail_total = trail_total + (trail * c - lead * s)
                turned[lead_rows, cols] = lead_total
                turned[trail_rows, cols] = trail_total

    @pl.when(group == groups - 1)
    def _():
        for at, total in enumerate(totals):
            if final:
                whole = total[...] * gain_ref[...] if at == 2 else total[...]
                outs[0][:, at * LANES : (at + 1) * LANES] = whole.T.astype(outs[0].dtype)
            else:
                outs[at][...] = total[...].astype(outs[at].dtype)


def added(*terms):
    return sum(term.astype(F32) for term in terms).astype(BF16)


def per_device(
    atom_devices, queries, keys, values, cotangent, positions, species, domain, species_gain,
    frequency, directions, dir_weight, dir_mask,
):
    atoms, feats = queries.shape
    index = lax.axis_index("atoms")[None].astype(jnp.int32)
    mine = lax.axis_index("dirs").astype(jnp.int32)
    vmem = pl.BlockSpec(memory_space=pltpu.VMEM)
    smem = pl.BlockSpec(memory_space=pltpu.SMEM)
    params = pltpu.CompilerParams(vmem_limit_bytes=VMEM_LIMIT)
    shape = jax.ShapeDtypeStruct

    qt, kt, vt, gt, gain = pl.pallas_call(
        prepare_kernel,
        in_specs=[smem] + [vmem] * 7,
        out_specs=[vmem] * 5,
        out_shape=[
            shape((feats, atoms), BF16), shape((feats, atoms), F32), shape((feats, atoms), BF16),
            shape((feats, atoms), BF16), shape((feats, atoms), F32),
        ],
        compiler_params=params,
        name="prepare",
    )(index, domain[None, :], species[None, :], species_gain, queries, keys, values, cotangent)

    part = min(256, atoms)

    def make_states(first, groups, after):
        sent = (2, QUADS, groups * 2 * QUARTER, feats)
        sent_spec = pl.BlockSpec((2, QUADS, 2 * QUARTER, feats), lambda g: (0, 0, g, 0))
        phase_spec = pl.BlockSpec((GROUP * QUARTER, atoms), lambda g: (g, 0))
        return pl.pallas_call(
            functools.partial(states_kernel, first, part, 1.0 / math.sqrt(feats * atoms)),
            grid=(groups,),
            in_specs=[smem] * 4 + [vmem] * 6 + [pl.BlockSpec(memory_space=pl.ANY)] * len(after),
            out_specs=[sent_spec] * 2 + [phase_spec] * 2,
            out_shape=[shape(sent, BF16)] * 2
            + [shape((groups * GROUP * QUARTER, atoms), BF16)] * 2,
            scratch_shapes=[
                pltpu.VMEM((WIDTH, atoms), BF16),
                pltpu.VMEM((WIDTH, atoms), BF16),
                pltpu.VMEM((2, 2, QUADS, 2 * QUARTER, feats), BF16),
            ],
            compiler_params=params,
            cost_estimate=pl.CostEstimate(
                flops=8 * groups * WIDTH * atoms * feats,
                bytes_accessed=2 * groups * WIDTH * atoms, transcendentals=0,
            ),
            name="states",
        )(
            index, directions, dir_weight, dir_mask, frequency[None, :], positions, qt, kt,
            values, cotangent, *after,
        )

    def moved(x, target):
        return lax.ppermute(x, "atoms", [(i, target(i)) for i in range(atom_devices)])

    def by_core(x):
        return moved(x, lambda i: i ^ 1)

    def by_pair(x):
        return moved(x, lambda i: i ^ 2)

    def by_quad(x, step):
        return moved(x, lambda i: (i & ~12) | ((((i >> 2) + step) & 3) << 2))

    def crossing(kept, sent):
        arrived = by_core(sent)
        return arrived, added(kept[1], arrived[1])

    def summed(kept, arrived, crossing_out):
        half = added(kept[0], arrived[0], by_pair(crossing_out))
        quarter = added(half[0], *(by_quad(half[step], step) for step in range(1, QUADS)))
        whole = quarter
        for step in range(16, atom_devices, 16):
            whole = added(whole, moved(quarter, lambda i: (i + step) % atom_devices))
        gathered = [whole] + [by_quad(whole, QUADS - step) for step in range(1, QUADS)]
        half = jnp.concatenate(gathered, axis=0)
        other = by_pair(half)
        return half, other, by_core(half), by_core(other)

    half_atoms = atoms // 2

    def mix(half, pieces, groups, phases, totals, final, dtype):
        blocks = 1 if final else 2
        mix_part = min(256, half_atoms)
        rows_all = pl.BlockSpec((feats, half_atoms), lambda n, g, index, half: (0, half[0] + n))
        phase_spec = pl.BlockSpec(
            (GROUP * QUARTER, half_atoms), lambda n, g, index, half: (g, half[0] + n)
        )
        operands = [*pieces, vt, gt, kt, qt, *phases]
        specs = [vmem] * 4 + [rows_all] * 4 + [phase_spec] * 2
        if final:
            operands.append(gain)
            specs.append(rows_all)
        if totals is not None:
            operands += totals
            specs += [rows_all] * 4
        scratch = [
            pltpu.VMEM((2, 2, QUADS, groups * 2 * QUARTER, feats), BF16),
            pltpu.VMEM((2, groups, WIDTH, feats), BF16),
            pltpu.VMEM((2, groups, feats, WIDTH), BF16),
        ] + [pltpu.VMEM((feats, half_atoms), F32)] * 4
        if final:
            out_specs = pl.BlockSpec(
                (half_atoms, 4 * feats), lambda n, g, index, half: (0, 0)
            )
            out_shape = shape((half_atoms, 4 * feats), dtype)
        else:
            out_specs = [rows_all] * 4
            out_shape = [shape((feats, atoms), dtype)] * 4
        return pl.pallas_call(
            functools.partial(mix_kernel, totals is not None, final, mix_part),
            grid_spec=pltpu.PrefetchScalarGridSpec(
                num_scalar_prefetch=2,
                grid=(blocks, groups),
                in_specs=specs,
                out_specs=out_specs,
                scratch_shapes=scratch,
            ),
            out_shape=out_shape,
            compiler_params=params,
            cost_estimate=pl.CostEstimate(
                flops=8 * groups * WIDTH * blocks * half_atoms * feats,
                bytes_accessed=2 * groups * WIDTH * blocks * half_atoms, transcendentals=0,
            ),
            name="mix",
        )(index, half[None], *operands)

    made = []
    first = 0
    for groups in CHUNKS:
        after = [made[-2][2]] if len(made) > 1 else []
        kept, sent, *phases = make_states(first, groups, after)
        made.append((kept, *crossing(kept, sent), phases, groups))
        first += groups
    totals = None
    for kept, arrived, crossing_out, phases, groups in made[:-1]:
        pieces = summed(kept, arrived, crossing_out)
        totals = mix(jnp.int32(0), pieces, groups, phases, totals, False, BF16)
    kept, arrived, crossing_out, phases, groups = made[-1]
    pieces = summed(kept, arrived, crossing_out)
    away = mix(1 - mine, pieces, groups, phases, totals, True, BF16)
    theirs = lax.ppermute(away, "dirs", [(0, 1), (1, 0)])
    ours = mix(mine, pieces, groups, phases, totals, True, F32)
    total = (ours + theirs.astype(F32)).astype(BF16)
    return tuple(total[:, at * feats : (at + 1) * feats] for at in range(4))


def solution(mesh):
    return jax.shard_map(
        functools.partial(per_device, mesh.shape["atoms"]),
        mesh=mesh,
        in_specs=(
            P("atoms", None),
            P("atoms", None),
            P("atoms", None),
            P("atoms", None),
            P(None, "atoms"),
            P("atoms"),
            P("atoms"),
            P(),
            P(),
            P(None, "dirs"),
            P("dirs"),
            P("dirs"),
        ),
        out_specs=(
            P(("atoms", "dirs"), None),
            P(("atoms", "dirs"), None),
            P(("atoms", "dirs"), None),
            P(("atoms", "dirs"), None),
        ),
        check_vma=False,
    )
```

```python
import functools
import math

import jax
import jax.numpy as jnp
from jax import lax
from jax.experimental import pallas as pl
from jax.experimental.pallas import tpu as pltpu
from jax.sharding import PartitionSpec as P

BF16 = jnp.bfloat16
F32 = jnp.float32
GROUP = 4
QUADS = 4
LANES = 128
QUARTER = LANES // QUADS
WIDTH = GROUP * LANES
VMEM_LIMIT = 56 * 2**20
CHUNKS = (4, 4, 3)

SIN_COEF = (4.4428679, -7.30744342, 3.59478808, -0.78437403)
COS_COEF = (1.41420408, -6.97764206, 5.71523839, -1.72834866)


def cos_sin_turns(turns):
    part = turns - jnp.round(turns)
    square = part * part
    sine = SIN_COEF[2] + square * SIN_COEF[3]
    sine = SIN_COEF[1] + square * sine
    sine = part * (SIN_COEF[0] + square * sine)
    cosine = COS_COEF[2] + square * COS_COEF[3]
    cosine = COS_COEF[1] + square * cosine
    cosine = COS_COEF[0] + square * cosine
    return 1.0 - sine * sine, sine * cosine


def column(row):
    size = row.shape[1]
    at_row = lax.broadcasted_iota(jnp.int32, (size, size), 0)
    at_lane = lax.broadcasted_iota(jnp.int32, (size, size), 1)
    return jnp.sum(jnp.where(at_row == at_lane, row, 0.0), axis=1, keepdims=True)


def place_of(index):
    return index & 1, (index >> 1) & 1, (index >> 2) & 3


def prepare_kernel(
    index_ref, domain_ref, species_ref, gain_ref, q_ref, k_ref, v_ref, g_ref,
    qt_ref, kt_ref, vt_ref, gt_ref, gain_out,
):
    alive = (domain_ref[...] == index_ref[0]).astype(F32)
    species = species_ref[...]
    gain = jnp.zeros(gain_out.shape, F32)
    for s in range(gain_ref.shape[0]):
        gain = jnp.where(species == s, column(gain_ref[s : s + 1, :]), gain)
    gain_out[...] = gain
    kt_ref[...] = k_ref[...].astype(F32).T * gain * alive
    qt_ref[...] = (q_ref[...].astype(F32).T * alive).astype(BF16)
    vt_ref[...] = (v_ref[...].astype(F32).T * alive).astype(BF16)
    gt_ref[...] = (g_ref[...].astype(F32).T * alive).astype(BF16)


def states_kernel(
    first, part, scale, slotted, index_ref, dirs_ref, weight_ref, mask_ref, freq_ref, pos_ref,
    qt_ref, kt_ref, v_ref, g_ref, *refs,
):
    if slotted:
        kept_ref, sent_ref, cos_ref, sin_ref, kr, qr, slots = refs[-7:]
    else:
        both_ref, cos_ref, sin_ref, kr, qr = refs[-5:]
    group = first + pl.program_id(0)
    atoms = pos_ref.shape[1]
    core, pair, quad = place_of(index_ref[0])
    freq = column(freq_ref[...]) * (1.0 / (2.0 * math.pi))
    for start in range(0, atoms, part):
        cols = slice(start, start + part)
        for i in range(GROUP):
            u = group * GROUP + i
            proj = (
                dirs_ref[0, u] * pos_ref[0:1, cols]
                + dirs_ref[1, u] * pos_ref[1:2, cols]
                + dirs_ref[2, u] * pos_ref[2:3, cols]
            )
            cosine, sine = cos_sin_turns(freq * proj)
            cos_ref[i * QUARTER : (i + 1) * QUARTER, cols] = cosine.astype(BF16)
            sin_ref[i * QUARTER : (i + 1) * QUARTER, cols] = sine.astype(BF16)
            for src, dst in ((kt_ref, kr), (qt_ref, qr)):
                for m in range(2):
                    lead = src[QUARTER * m : QUARTER * (m + 1), cols].astype(F32)
                    trail = src[QUARTER * (m + 2) : QUARTER * (m + 3), cols].astype(F32)
                    row = i * LANES + QUARTER * m
                    dst[row : row + QUARTER, cols] = (lead * cosine - trail * sine).astype(BF16)
                    row = row + 2 * QUARTER
                    dst[row : row + QUARTER, cols] = (lead * sine + trail * cosine).astype(BF16)

    for kind, rot, other in ((0, kr, v_ref), (1, qr, g_ref)):
        total = jnp.dot(rot[...], other[...], preferred_element_type=F32)
        for i in range(GROUP):
            u = group * GROUP + i
            coef = weight_ref[u] * mask_ref[u].astype(F32) * scale
            rows = slice(i % 2 * QUARTER, (i % 2 + 1) * QUARTER)
            for m in range(QUADS):
                row = i * LANES + m * QUARTER
                scaled = (total[row : row + QUARTER, :] * coef).astype(BF16)
                if slotted:
                    slots[kind ^ core, (i // 2) ^ pair, (m - quad) & 3, rows, :] = scaled
                else:
                    both_ref[kind, row : row + QUARTER, :] = scaled
    if slotted:
        kept_ref[...] = slots[0]
        sent_ref[...] = slots[1]


def rotated(x, cosine, sine):
    pieces = []
    for i in range(GROUP):
        c = cosine[i * QUARTER : (i + 1) * QUARTER]
        s = sine[i * QUARTER : (i + 1) * QUARTER]
        quarters = [x[m * QUARTER : (m + 1) * QUARTER] for m in range(QUADS)]
        pieces += [quarters[m] * c - quarters[m + 2] * s for m in range(2)]
        pieces += [quarters[m] * s + quarters[m + 2] * c for m in range(2)]
    return jnp.concatenate(pieces, axis=0)


def mix_kernel(
    slotted, has_totals, final, part, index_ref, half_ref, *refs,
):
    del half_ref
    refs = list(refs)
    source_count = 4 if slotted else 1
    sources, refs = refs[:source_count], refs[source_count:]
    vt_ref, gt_ref, kt_ref, qt_ref, cos_ref, sin_ref = refs[:6]
    refs = refs[6:]
    if final:
        gain_ref, refs = refs[0], refs[1:]
    if has_totals:
        before, refs = refs[:4], refs[4:]
    out_count = 1 if final else 4
    outs, refs = refs[:out_count], refs[out_count:]
    states, states_t = refs[:2]
    totals = refs[2:6]
    slots = refs[6] if slotted else None
    group = pl.program_id(0)
    groups = pl.num_programs(0)
    core, pair, quad = place_of(index_ref[0])

    @pl.when(group == 0)
    def _():
        for at, source in enumerate(sources):
            if slotted:
                slots[at // 2, at % 2] = source[...].reshape(slots.shape[2:])
            else:
                states[...] = source[...].reshape(states.shape)
        for g in range(states.shape[1]):
            for kind in range(2):
                for i in range(GROUP):
                    start = g * 2 * QUARTER + i % 2 * QUARTER
                    for m in range(QUADS if slotted else 0):
                        row = i * LANES + m * QUARTER
                        states[kind, g, row : row + QUARTER, :] = slots[
                            kind ^ core, (i // 2) ^ pair, (m - quad) & 3,
                            start : start + QUARTER, :,
                        ]
                    whole = states[kind, g, i * LANES : (i + 1) * LANES, :]
                    states_t[kind, g, :, i * LANES : (i + 1) * LANES] = (
                        whole.astype(F32).T.astype(BF16)
                    )

    @pl.when(group == 0)
    def _():
        for at, total in enumerate(totals):
            total[...] = before[at][...].astype(F32) if has_totals else jnp.zeros_like(total)

    for start in range(0, vt_ref.shape[1], part):
        cols = slice(start, start + part)
        cosine = cos_ref[:, cols]
        sine = sin_ref[:, cols]
        for kind, x_ref, direct in ((0, qt_ref, totals[0]), (1, kt_ref, totals[3])):
            turned = rotated(x_ref[:, cols].astype(BF16), cosine, sine)
            direct[:, cols] += jnp.dot(states_t[kind, group], turned, preferred_element_type=F32)
        cosine = cosine.astype(F32)
        sine = sine.astype(F32)
        for kind, fixed, turned in ((0, gt_ref, totals[1]), (1, vt_ref, totals[2])):
            back = jnp.dot(states[kind, group], fixed[:, cols], preferred_element_type=F32)
            for m in range(2):
                lead_rows = slice(QUARTER * m, QUARTER * (m + 1))
                trail_rows = slice(QUARTER * (m + 2), QUARTER * (m + 3))
                lead_total = turned[lead_rows, cols]
                trail_total = turned[trail_rows, cols]
                for i in range(GROUP):
                    c = cosine[i * QUARTER : (i + 1) * QUARTER]
                    s = sine[i * QUARTER : (i + 1) * QUARTER]
                    row = i * LANES + QUARTER * m
                    lead = back[row : row + QUARTER, :]
                    trail = back[row + 2 * QUARTER : row + 3 * QUARTER, :]
                    lead_total = lead_total + (lead * c + trail * s)
                    trail_total = trail_total + (trail * c - lead * s)
                turned[lead_rows, cols] = lead_total
                turned[trail_rows, cols] = trail_total

    @pl.when(group == groups - 1)
    def _():
        for at, total in enumerate(totals):
            if final:
                whole = total[...] * gain_ref[...] if at == 2 else total[...]
                outs[0][:, at * LANES : (at + 1) * LANES] = whole.T.astype(outs[0].dtype)
            else:
                outs[at][...] = total[...].astype(outs[at].dtype)


def added(*terms):
    return sum(term.astype(F32) for term in terms).astype(BF16)


def per_device(
    atom_devices, queries, keys, values, cotangent, positions, species, domain, species_gain,
    frequency, directions, dir_weight, dir_mask,
):
    atoms, feats = queries.shape
    index = lax.axis_index("atoms")[None].astype(jnp.int32)
    mine = lax.axis_index("dirs").astype(jnp.int32)
    vmem = pl.BlockSpec(memory_space=pltpu.VMEM)
    smem = pl.BlockSpec(memory_space=pltpu.SMEM)
    params = pltpu.CompilerParams(vmem_limit_bytes=VMEM_LIMIT)
    shape = jax.ShapeDtypeStruct

    qt, kt, vt, gt, gain = pl.pallas_call(
        prepare_kernel,
        in_specs=[smem] + [vmem] * 7,
        out_specs=[vmem] * 5,
        out_shape=[
            shape((feats, atoms), BF16), shape((feats, atoms), F32), shape((feats, atoms), BF16),
            shape((feats, atoms), BF16), shape((feats, atoms), F32),
        ],
        compiler_params=params,
        name="prepare",
    )(index, domain[None, :], species[None, :], species_gain, queries, keys, values, cotangent)

    part = min(256, atoms)

    def make_states(first, groups, slotted, after=()):
        phase_spec = pl.BlockSpec((GROUP * QUARTER, atoms), lambda g: (g, 0))
        if slotted:
            sent = [shape((2, QUADS, groups * 2 * QUARTER, feats), BF16)] * 2
            sent_spec = [pl.BlockSpec((2, QUADS, 2 * QUARTER, feats), lambda g: (0, 0, g, 0))] * 2
            slots = [pltpu.VMEM((2, 2, QUADS, 2 * QUARTER, feats), BF16)]
        else:
            sent = [shape((2, groups * WIDTH, feats), BF16)]
            sent_spec = [pl.BlockSpec((2, WIDTH, feats), lambda g: (0, g, 0))]
            slots = []
        return pl.pallas_call(
            functools.partial(
                states_kernel, first, part, 1.0 / math.sqrt(feats * atoms), slotted
            ),
            grid=(groups,),
            in_specs=[smem] * 4 + [vmem] * 6 + [pl.BlockSpec(memory_space=pl.ANY)] * len(after),
            out_specs=sent_spec + [phase_spec] * 2,
            out_shape=sent + [shape((groups * GROUP * QUARTER, atoms), BF16)] * 2,
            scratch_shapes=[
                pltpu.VMEM((WIDTH, atoms), BF16),
                pltpu.VMEM((WIDTH, atoms), BF16),
            ]
            + slots,
            compiler_params=params,
            cost_estimate=pl.CostEstimate(
                flops=8 * groups * WIDTH * atoms * feats,
                bytes_accessed=2 * groups * WIDTH * atoms, transcendentals=0,
            ),
            name="states",
        )(
            index, directions, dir_weight, dir_mask, frequency[None, :], positions, qt, kt,
            values, cotangent, *after,
        )

    def moved(x, target):
        return lax.ppermute(x, "atoms", [(i, target(i)) for i in range(atom_devices)])

    def by_core(x):
        return moved(x, lambda i: i ^ 1)

    def by_pair(x):
        return moved(x, lambda i: i ^ 2)

    def by_quad(x, step):
        return moved(x, lambda i: (i & ~12) | ((((i >> 2) + step) & 3) << 2))

    def crossing(kept, sent):
        arrived = by_core(sent)
        return arrived, added(kept[1], arrived[1])

    def summed(kept, arrived, crossing_out):
        half = added(kept[0], arrived[0], by_pair(crossing_out))
        quarter = added(half[0], *(by_quad(half[step], step) for step in range(1, QUADS)))
        whole = quarter
        for step in range(16, atom_devices, 16):
            whole = added(whole, moved(quarter, lambda i: (i + step) % atom_devices))
        gathered = [whole] + [by_quad(whole, QUADS - step) for step in range(1, QUADS)]
        half = jnp.concatenate(gathered, axis=0)
        other = by_pair(half)
        return half, other, by_core(half), by_core(other)

    half_atoms = atoms // 2

    def mix(half, pieces, groups, phases, totals, final, dtype):
        slotted = len(pieces) == 4
        rows_half = pl.BlockSpec((feats, half_atoms), lambda g, index, half: (0, half[0]))
        phase_spec = pl.BlockSpec(
            (GROUP * QUARTER, half_atoms), lambda g, index, half: (g, half[0])
        )
        totals_spec = pl.BlockSpec((feats, half_atoms), lambda g, index, half: (0, 0))
        operands = [*pieces, vt, gt, kt, qt, *phases]
        specs = [vmem] * len(pieces) + [rows_half] * 4 + [phase_spec] * 2
        if final:
            operands.append(gain)
            specs.append(rows_half)
        if totals is not None:
            operands += totals
            specs += [totals_spec] * 4
        scratch = [
            pltpu.VMEM((2, groups, WIDTH, feats), BF16),
            pltpu.VMEM((2, groups, feats, WIDTH), BF16),
        ] + [pltpu.VMEM((feats, half_atoms), F32)] * 4
        if slotted:
            scratch.append(pltpu.VMEM((2, 2, QUADS, groups * 2 * QUARTER, feats), BF16))
        if final:
            out_specs = pl.BlockSpec((half_atoms, 4 * feats), lambda g, index, half: (0, 0))
            out_shape = shape((half_atoms, 4 * feats), dtype)
        else:
            out_specs = [totals_spec] * 4
            out_shape = [shape((feats, half_atoms), dtype)] * 4
        return pl.pallas_call(
            functools.partial(
                mix_kernel, slotted, totals is not None, final, min(256, half_atoms)
            ),
            grid_spec=pltpu.PrefetchScalarGridSpec(
                num_scalar_prefetch=2,
                grid=(groups,),
                in_specs=specs,
                out_specs=out_specs,
                scratch_shapes=scratch,
            ),
            out_shape=out_shape,
            compiler_params=params,
            cost_estimate=pl.CostEstimate(
                flops=8 * groups * WIDTH * half_atoms * feats,
                bytes_accessed=2 * groups * WIDTH * half_atoms, transcendentals=0,
            ),
            name="mix",
        )(index, half[None], *operands)

    def after(x, *others):
        return pl.pallas_call(
            lambda x_ref, *refs: refs[-1].__setitem__(..., x_ref[...]),
            in_specs=[vmem] + [pl.BlockSpec(memory_space=pl.ANY)] * len(others),
            out_specs=vmem,
            out_shape=shape(x.shape, x.dtype),
            name="after",
        )(x, *others)

    bounds = [sum(CHUNKS[:at]) for at in range(len(CHUNKS))]
    both, *phases = make_states(bounds[0], CHUNKS[0], False)
    made = [phases]
    shard = lax.psum_scatter(
        both.reshape(-1, feats), "atoms", scatter_dimension=0, tiled=True
    )
    kept, sent, *phases = make_states(bounds[1], CHUNKS[1], True, [both])
    made.append(phases)
    crossed = [(kept, *crossing(kept, sent))]
    kept, sent, *phases = make_states(bounds[2], CHUNKS[2], True, [crossed[0][2]])
    made.append(phases)
    crossed.append((kept, *crossing(kept, sent)))
    shard = after(shard, sent)
    pieces = [[lax.all_gather(shard, "atoms", axis=0, tiled=True)]]
    pieces += [summed(*each) for each in crossed]

    def mix_all(half, dtype):
        totals = None
        for at, groups in enumerate(CHUNKS):
            final = at == len(CHUNKS) - 1
            totals = mix(
                half, pieces[at], groups, made[at], totals, final, dtype if final else BF16
            )
        return totals

    theirs = lax.ppermute(mix_all(1 - mine, BF16), "dirs", [(0, 1), (1, 0)])
    total = (mix_all(mine, F32) + theirs.astype(F32)).astype(BF16)
    return tuple(total[:, at * feats : (at + 1) * feats] for at in range(4))


def solution(mesh):
    return jax.shard_map(
        functools.partial(per_device, mesh.shape["atoms"]),
        mesh=mesh,
        in_specs=(
            P("atoms", None),
            P("atoms", None),
            P("atoms", None),
            P("atoms", None),
            P(None, "atoms"),
            P("atoms"),
            P("atoms"),
            P(),
            P(),
            P(None, "dirs"),
            P("dirs"),
            P("dirs"),
        ),
        out_specs=(
            P(("atoms", "dirs"), None),
            P(("atoms", "dirs"), None),
            P(("atoms", "dirs"), None),
            P(("atoms", "dirs"), None),
        ),
        check_vma=False,
    )
```

```python
import functools
import math

import jax
import jax.numpy as jnp
from jax import lax
from jax.experimental import pallas as pl
from jax.experimental.pallas import tpu as pltpu
from jax.sharding import PartitionSpec as P

BF16 = jnp.bfloat16
F32 = jnp.float32
GROUP = 4
QUADS = 4
LANES = 128
QUARTER = LANES // QUADS
WIDTH = GROUP * LANES
VMEM_LIMIT = 30 * 2**20
EARLY = 6
PIECES = (1, 2, 2)
MIX_PIECES = (3, 3)

SIN_COEF = (4.4428679, -7.30744342, 3.59478808, -0.78437403)
COS_COEF = (1.41420408, -6.97764206, 5.71523839, -1.72834866)


def cos_sin_turns(turns):
    part = turns - jnp.round(turns)
    square = part * part
    sine = SIN_COEF[2] + square * SIN_COEF[3]
    sine = SIN_COEF[1] + square * sine
    sine = part * (SIN_COEF[0] + square * sine)
    cosine = COS_COEF[2] + square * COS_COEF[3]
    cosine = COS_COEF[1] + square * cosine
    cosine = COS_COEF[0] + square * cosine
    return 1.0 - sine * sine, sine * cosine


def column(row):
    size = row.shape[1]
    at_row = lax.broadcasted_iota(jnp.int32, (size, size), 0)
    at_lane = lax.broadcasted_iota(jnp.int32, (size, size), 1)
    return jnp.sum(jnp.where(at_row == at_lane, row, 0.0), axis=1, keepdims=True)


def place_of(index):
    return index & 1, (index >> 1) & 1, (index >> 2) & 3


def prepare_kernel(
    index_ref, domain_in, species_in, gain_in, q_in, k_in, v_in, g_in,
    qt_ref, kt_ref, kt_half, vt_ref, gt_ref, gain_out, v_ref, g_ref,
    domain_ref, species_ref, gain_ref, q_ref, k_ref, sems,
):
    copies = [
        pltpu.make_async_copy(source, target, sems.at[at])
        for at, (source, target) in enumerate(
            (
                (domain_in, domain_ref), (species_in, species_ref), (gain_in, gain_ref),
                (k_in, k_ref), (q_in, q_ref), (v_in, v_ref), (g_in, g_ref),
            )
        )
    ]
    for copy in copies:
        copy.start()
    for copy in copies[:4]:
        copy.wait()
    alive = (domain_ref[...] == index_ref[0]).astype(F32)
    species = species_ref[...]
    gain = jnp.zeros(gain_out.shape, F32)
    for s in range(gain_ref.shape[0]):
        gain = jnp.where(species == s, column(gain_ref[s : s + 1, :]), gain)
    gain_out[...] = gain
    gained = k_ref[...].astype(F32).T * gain * alive
    kt_ref[...] = gained
    kt_half[...] = gained.astype(BF16)
    copies[4].wait()
    qt_ref[...] = (q_ref[...].astype(F32).T * alive).astype(BF16)
    copies[5].wait()
    vt_ref[...] = (v_ref[...].astype(F32).T * alive).astype(BF16)
    copies[6].wait()
    gt_ref[...] = (g_ref[...].astype(F32).T * alive).astype(BF16)


def states_kernel(
    first, part, scale, index_ref, dirs_ref, weight_ref, mask_ref, freq_ref, pos_ref,
    qt_ref, kt_ref, v_ref, g_ref, *refs,
):
    kept_ref, sent_ref, cos_ref, sin_ref, kr, qr, slots = refs[-7:]
    group = first + pl.program_id(0)
    atoms = pos_ref.shape[1]
    core, pair, quad = place_of(index_ref[0])
    freq = column(freq_ref[...]) * (1.0 / (2.0 * math.pi))
    for start in range(0, atoms, part):
        cols = slice(start, start + part)
        for i in range(GROUP):
            u = group * GROUP + i
            proj = (
                dirs_ref[0, u] * pos_ref[0:1, cols]
                + dirs_ref[1, u] * pos_ref[1:2, cols]
                + dirs_ref[2, u] * pos_ref[2:3, cols]
            )
            cosine, sine = cos_sin_turns(freq * proj)
            cos_ref[i * QUARTER : (i + 1) * QUARTER, cols] = cosine.astype(BF16)
            sin_ref[i * QUARTER : (i + 1) * QUARTER, cols] = sine.astype(BF16)
            for src, dst in ((kt_ref, kr), (qt_ref, qr)):
                for m in range(2):
                    lead = src[QUARTER * m : QUARTER * (m + 1), cols].astype(F32)
                    trail = src[QUARTER * (m + 2) : QUARTER * (m + 3), cols].astype(F32)
                    row = i * LANES + QUARTER * m
                    dst[row : row + QUARTER, cols] = (lead * cosine - trail * sine).astype(BF16)
                    row = row + 2 * QUARTER
                    dst[row : row + QUARTER, cols] = (lead * sine + trail * cosine).astype(BF16)

    for kind, rot, other in ((0, kr, v_ref), (1, qr, g_ref)):
        total = jnp.dot(rot[...], other[...], preferred_element_type=F32)
        for i in range(GROUP):
            u = group * GROUP + i
            coef = weight_ref[u] * mask_ref[u].astype(F32) * scale
            rows = slice(i % 2 * QUARTER, (i % 2 + 1) * QUARTER)
            for m in range(QUADS):
                row = i * LANES + m * QUARTER
                slots[kind ^ core, (i // 2) ^ pair, (m - quad) & 3, rows, :] = (
                    total[row : row + QUARTER, :] * coef
                ).astype(BF16)
    kept_ref[...] = slots[0]
    sent_ref[...] = slots[1]


def rotated(x, cosine, sine):
    pieces = []
    for i in range(GROUP):
        c = cosine[i * QUARTER : (i + 1) * QUARTER]
        s = sine[i * QUARTER : (i + 1) * QUARTER]
        quarters = [x[m * QUARTER : (m + 1) * QUARTER] for m in range(QUADS)]
        pieces += [quarters[m] * c - quarters[m + 2] * s for m in range(2)]
        pieces += [quarters[m] * s + quarters[m + 2] * c for m in range(2)]
    return jnp.concatenate(pieces, axis=0)


def mix_kernel(
    first, has_totals, final, part, index_ref, half_ref, *refs,
):
    del half_ref
    refs = list(refs)
    sources, refs = refs[:4], refs[4:]
    vt_ref, gt_ref, kt_ref, qt_ref, cos_ref, sin_ref = refs[:6]
    refs = refs[6:]
    if final:
        gain_ref, refs = refs[0], refs[1:]
    if has_totals:
        before, refs = refs[:4], refs[4:]
    out_count = 1 if final else 4
    outs, refs = refs[-7 - out_count : -7], refs[-7:]
    states, states_t, slots = refs[:3]
    totals = refs[3:]
    group = pl.program_id(0)
    groups = pl.num_programs(0)
    core, pair, quad = place_of(index_ref[0])

    @pl.when(group == 0)
    def _():
        for at, source in enumerate(sources):
            slots[at // 2, at % 2] = source[...].reshape(slots.shape[2:])
        for g in range(states.shape[1]):
            for kind in range(2):
                for i in range(GROUP):
                    start = (first + g) * 2 * QUARTER + i % 2 * QUARTER
                    for m in range(QUADS):
                        row = i * LANES + m * QUARTER
                        states[kind, g, row : row + QUARTER, :] = slots[
                            kind ^ core, (i // 2) ^ pair, (m - quad) & 3,
                            start : start + QUARTER, :,
                        ]
                    whole = states[kind, g, i * LANES : (i + 1) * LANES, :]
                    states_t[kind, g, :, i * LANES : (i + 1) * LANES] = (
                        whole.astype(F32).T.astype(BF16)
                    )

    @pl.when(group == 0)
    def _():
        for at, total in enumerate(totals):
            total[...] = before[at][...].astype(F32) if has_totals else jnp.zeros_like(total)

    for start in range(0, vt_ref.shape[1], part):
        cols = slice(start, start + part)
        cosine = cos_ref[:, cols]
        sine = sin_ref[:, cols]
        for kind, x_ref, direct in ((0, qt_ref, totals[0]), (1, kt_ref, totals[3])):
            turned = rotated(x_ref[:, cols], cosine, sine)
            direct[:, cols] += jnp.dot(states_t[kind, group], turned, preferred_element_type=F32)
        cosine = cosine.astype(F32)
        sine = sine.astype(F32)
        for kind, fixed, turned in ((0, gt_ref, totals[1]), (1, vt_ref, totals[2])):
            back = jnp.dot(states[kind, group], fixed[:, cols], preferred_element_type=F32)
            for m in range(2):
                lead_rows = slice(QUARTER * m, QUARTER * (m + 1))
                trail_rows = slice(QUARTER * (m + 2), QUARTER * (m + 3))
                lead_total = turned[lead_rows, cols]
                trail_total = turned[trail_rows, cols]
                for i in range(GROUP):
                    c = cosine[i * QUARTER : (i + 1) * QUARTER]
                    s = sine[i * QUARTER : (i + 1) * QUARTER]
                    row = i * LANES + QUARTER * m
                    lead = back[row : row + QUARTER, :]
                    trail = back[row + 2 * QUARTER : row + 3 * QUARTER, :]
                    lead_total = lead_total + (lead * c + trail * s)
                    trail_total = trail_total + (trail * c - lead * s)
                turned[lead_rows, cols] = lead_total
                turned[trail_rows, cols] = trail_total

    @pl.when(group == groups - 1)
    def _():
        for at, total in enumerate(totals):
            if final:
                whole = total[...] * gain_ref[...] if at == 2 else total[...]
                outs[0][:, at * LANES : (at + 1) * LANES] = whole.T.astype(outs[0].dtype)
            else:
                outs[at][...] = total[...].astype(outs[at].dtype)


def add_kernel(picks, count, *refs):
    total = sum(
        (ref[...] if at is None else ref[at]).astype(F32) for at, ref in zip(picks, refs)
    )
    refs[-1][...] = total.astype(BF16)


def join_kernel(count, *refs):
    size = refs[0].shape[0]
    for at in range(count):
        refs[-1][at * size : (at + 1) * size, :] = refs[at][...]


def per_device(
    atom_devices, queries, keys, values, cotangent, positions, species, domain, species_gain,
    frequency, directions, dir_weight, dir_mask,
):
    atoms, feats = queries.shape
    total_groups = dir_weight.shape[0] // GROUP
    late = total_groups - EARLY
    half_atoms = atoms // 2
    index = lax.axis_index("atoms")[None].astype(jnp.int32)
    mine = lax.axis_index("dirs").astype(jnp.int32)
    vmem = pl.BlockSpec(memory_space=pltpu.VMEM)
    smem = pl.BlockSpec(memory_space=pltpu.SMEM)
    hbm = pl.BlockSpec(memory_space=pltpu.HBM)
    anywhere = pl.BlockSpec(memory_space=pl.ANY)
    params = pltpu.CompilerParams(vmem_limit_bytes=VMEM_LIMIT)
    shape = jax.ShapeDtypeStruct

    qt, kt, kt_half, vt, gt, gain, v_near, g_near = pl.pallas_call(
        prepare_kernel,
        in_specs=[smem] + [hbm] * 7,
        out_specs=[vmem] * 8,
        out_shape=[
            shape((feats, atoms), BF16), shape((feats, atoms), F32), shape((feats, atoms), BF16),
            shape((feats, atoms), BF16), shape((feats, atoms), BF16), shape((feats, atoms), F32),
            shape((atoms, feats), BF16), shape((atoms, feats), BF16),
        ],
        scratch_shapes=[
            pltpu.VMEM((1, atoms), jnp.int32),
            pltpu.VMEM((1, atoms), jnp.int32),
            pltpu.VMEM(species_gain.shape, F32),
            pltpu.VMEM((atoms, feats), BF16),
            pltpu.VMEM((atoms, feats), BF16),
            pltpu.SemaphoreType.DMA((7,)),
        ],
        compiler_params=params,
        name="prepare",
    )(index, domain[None, :], species[None, :], species_gain, queries, keys, values, cotangent)

    def make_states(first, groups, offset, size, after=(), into=()):
        sent = shape((2, QUADS, size * 2 * QUARTER, feats), BF16)
        sent_spec = pl.BlockSpec(
            (2, QUADS, 2 * QUARTER, feats), lambda g: (0, 0, g + offset, 0)
        )
        phase = pltpu.HBM((size * GROUP * QUARTER, atoms), BF16)
        phase_spec = pl.BlockSpec((GROUP * QUARTER, atoms), lambda g: (g + offset, 0))
        operands = [
            index, directions, dir_weight, dir_mask, frequency[None, :], positions, qt, kt,
            v_near, g_near, *after,
        ]
        return pl.pallas_call(
            functools.partial(states_kernel, first, min(256, atoms), 1.0 / math.sqrt(feats * atoms)),
            grid=(groups,),
            in_specs=[smem] * 4 + [vmem] * 6 + [anywhere] * (len(after) + len(into)),
            out_specs=[sent_spec] * 2 + [phase_spec] * 2,
            out_shape=[sent] * 2 + [phase] * 2,
            input_output_aliases={len(operands) + at: at for at in range(len(into))},
            scratch_shapes=[
                pltpu.VMEM((WIDTH, atoms), BF16),
                pltpu.VMEM((WIDTH, atoms), BF16),
                pltpu.VMEM((2, 2, QUADS, 2 * QUARTER, feats), BF16),
            ],
            compiler_params=params,
            cost_estimate=pl.CostEstimate(
                flops=8 * groups * WIDTH * atoms * feats,
                bytes_accessed=2 * groups * WIDTH * atoms, transcendentals=0,
            ),
            name="states",
        )(*operands, *into)

    def moved(x, target):
        return lax.ppermute(x, "atoms", [(i, target(i)) for i in range(atom_devices)])

    def by_core(x):
        return moved(x, lambda i: i ^ 1)

    def by_pair(x):
        return moved(x, lambda i: i ^ 2)

    def by_quad(x, step):
        return moved(x, lambda i: (i & ~12) | ((((i >> 2) + step) & 3) << 2))

    def added(terms, after=()):
        first, at = terms[0]
        out = first.shape if at is None else first.shape[1:]
        return pl.pallas_call(
            functools.partial(add_kernel, [pick for _, pick in terms], len(terms)),
            in_specs=[vmem] * len(terms) + [anywhere] * len(after),
            out_specs=vmem,
            out_shape=shape(out, BF16),
            name="add",
        )(*(x for x, _ in terms), *after)

    def joined(parts, after=()):
        return pl.pallas_call(
            functools.partial(join_kernel, len(parts)),
            in_specs=[vmem] * len(parts) + [anywhere] * len(after),
            out_specs=vmem,
            out_shape=shape((len(parts) * parts[0].shape[0], feats), BF16),
            name="join",
        )(*parts, *after)

    def quarters(half):
        return [(half, 0)] + [(by_quad(half[step], step), None) for step in range(1, QUADS)]

    def whole_of(quarter):
        terms = [(quarter, None)]
        for step in range(16, atom_devices, 16):
            terms.append((moved(quarter, lambda i: (i + step) % atom_devices), None))
        return added(terms) if len(terms) > 1 else quarter

    def spread(whole):
        return [whole] + [by_quad(whole, QUADS - step) for step in range(1, QUADS)]

    def shared(half):
        other = by_pair(half)
        return half, other, by_core(half), by_core(other)

    def mix(half, pieces, first, groups, phases, totals, final, dtype, after=()):
        rows_half = pl.BlockSpec((feats, half_atoms), lambda g, index, half: (0, half[0]))
        phase_spec = pl.BlockSpec(
            (GROUP * QUARTER, half_atoms), lambda g, index, half: (g + first, half[0])
        )
        totals_spec = pl.BlockSpec((feats, half_atoms), lambda g, index, half: (0, 0))
        operands = [*pieces, vt, gt, kt_half, qt, *phases]
        specs = [vmem] * 4 + [rows_half] * 4 + [phase_spec] * 2
        if final:
            operands.append(gain)
            specs.append(rows_half)
        if totals is not None:
            operands += totals
            specs += [totals_spec] * 4
        slot_rows = pieces[0].shape[0] // QUADS
        if final:
            out_specs = pl.BlockSpec((half_atoms, 4 * feats), lambda g, index, half: (0, 0))
            out_shape = shape((half_atoms, 4 * feats), dtype)
        else:
            out_specs = [totals_spec] * 4
            out_shape = [shape((feats, half_atoms), BF16)] * 4
        return pl.pallas_call(
            functools.partial(
                mix_kernel, first, totals is not None, final, min(256, half_atoms)
            ),
            grid_spec=pltpu.PrefetchScalarGridSpec(
                num_scalar_prefetch=2,
                grid=(groups,),
                in_specs=specs + [anywhere] * len(after),
                out_specs=out_specs,
                scratch_shapes=[
                    pltpu.VMEM((2, groups, WIDTH, feats), BF16),
                    pltpu.VMEM((2, groups, feats, WIDTH), BF16),
                    pltpu.VMEM((2, 2, QUADS, slot_rows, feats), BF16),
                ]
                + [pltpu.VMEM((feats, half_atoms), F32)] * 4,
            ),
            out_shape=out_shape,
            compiler_params=params,
            cost_estimate=pl.CostEstimate(
                flops=8 * groups * WIDTH * half_atoms * feats,
                bytes_accessed=2 * groups * WIDTH * half_atoms, transcendentals=0,
            ),
            name="mix",
        )(index, half[None], *operands, *after)

    kept0, sent0, *phases0 = make_states(0, EARLY, 0, EARLY)
    arrived0 = by_core(sent0)
    made = make_states(EARLY, PIECES[0], 0, late, [sent0])
    cross0 = added([(kept0, 1), (arrived0, 1)], [made[0]])
    crossed0 = by_pair(cross0)
    made = make_states(EARLY + PIECES[0], PIECES[1], PIECES[0], late, [cross0], made)
    half0 = added([(kept0, 0), (arrived0, 0), (crossed0, None)], [made[0]])
    quarters0 = quarters(half0)
    done = PIECES[0] + PIECES[1]
    kept1, sent1, *phases1 = make_states(
        EARLY + done, late - done, done, late, [half0], made
    )
    arrived1 = by_core(sent1)
    whole0 = whole_of(added(quarters0, [sent1]))
    spread0 = spread(whole0)
    cross1 = added([(kept1, 1), (arrived1, 1)], [whole0])
    crossed1 = by_pair(cross1)
    pieces0 = shared(joined(spread0, [cross1]))
    half1 = added([(kept1, 0), (arrived1, 0), (crossed1, None)], [pieces0[0]])
    whole1 = whole_of(added(quarters(half1)))
    spread1 = spread(whole1)
    away = 1 - mine
    totals = mix(away, pieces0, 0, MIX_PIECES[0], phases0, None, False, BF16, [whole1])
    pieces1 = shared(joined(spread1, [totals[0]]))
    totals = mix(
        away, pieces0, MIX_PIECES[0], EARLY - MIX_PIECES[0], phases0, totals, False, BF16,
        [pieces1[0]],
    )
    sent = mix(away, pieces1, 0, late, phases1, totals, True, BF16)
    theirs = lax.ppermute(sent, "dirs", [(0, 1), (1, 0)])
    totals = mix(mine, pieces0, 0, EARLY, phases0, None, False, BF16, [sent])
    ours = mix(mine, pieces1, 0, late, phases1, totals, True, F32)
    total = (ours + theirs.astype(F32)).astype(BF16)
    return tuple(total[:, at * feats : (at + 1) * feats] for at in range(4))


def solution(mesh):
    return jax.shard_map(
        functools.partial(per_device, mesh.shape["atoms"]),
        mesh=mesh,
        in_specs=(
            P("atoms", None),
            P("atoms", None),
            P("atoms", None),
            P("atoms", None),
            P(None, "atoms"),
            P("atoms"),
            P("atoms"),
            P(),
            P(),
            P(None, "dirs"),
            P("dirs"),
            P("dirs"),
        ),
        out_specs=(
            P(("atoms", "dirs"), None),
            P(("atoms", "dirs"), None),
            P(("atoms", "dirs"), None),
            P(("atoms", "dirs"), None),
        ),
        check_vma=False,
    )
```

```python
import functools
import math

import jax
import jax.numpy as jnp
from jax import lax
from jax.experimental import pallas as pl
from jax.experimental.pallas import tpu as pltpu
from jax.sharding import PartitionSpec as P

BF16 = jnp.bfloat16
F32 = jnp.float32
GROUP = 4
QUADS = 4
LANES = 128
QUARTER = LANES // QUADS
WIDTH = GROUP * LANES
VMEM_LIMIT = 56 * 2**20
CHUNKS = (4, 4, 3)

SIN_COEF = (4.4428679, -7.30744342, 3.59478808, -0.78437403)
COS_COEF = (1.41420408, -6.97764206, 5.71523839, -1.72834866)


def cos_sin_turns(turns):
    part = turns - jnp.round(turns)
    square = part * part
    sine = SIN_COEF[2] + square * SIN_COEF[3]
    sine = SIN_COEF[1] + square * sine
    sine = part * (SIN_COEF[0] + square * sine)
    cosine = COS_COEF[2] + square * COS_COEF[3]
    cosine = COS_COEF[1] + square * cosine
    cosine = COS_COEF[0] + square * cosine
    return 1.0 - sine * sine, sine * cosine


def column(row):
    size = row.shape[1]
    at_row = lax.broadcasted_iota(jnp.int32, (size, size), 0)
    at_lane = lax.broadcasted_iota(jnp.int32, (size, size), 1)
    return jnp.sum(jnp.where(at_row == at_lane, row, 0.0), axis=1, keepdims=True)


def place_of(index):
    return index & 1, (index >> 1) & 1, (index >> 2) & 3


def slot_of(block, quad):
    away = block ^ quad
    return ((away & 1) << 1) | (away >> 1)


def prepare_kernel(
    index_ref, domain_ref, species_ref, gain_ref, q_ref, k_ref, v_ref, g_ref,
    qt_ref, kt_ref, vt_ref, gt_ref, gain_out,
):
    alive = (domain_ref[...] == index_ref[0]).astype(F32)
    species = species_ref[...]
    gain = jnp.zeros(gain_out.shape, F32)
    for s in range(gain_ref.shape[0]):
        gain = jnp.where(species == s, column(gain_ref[s : s + 1, :]), gain)
    gain_out[...] = gain
    kt_ref[...] = (k_ref[...].astype(F32).T * gain * alive).astype(BF16)
    qt_ref[...] = (q_ref[...].astype(F32).T * alive).astype(BF16)
    vt_ref[...] = (v_ref[...].astype(F32).T * alive).astype(BF16)
    gt_ref[...] = (g_ref[...].astype(F32).T * alive).astype(BF16)


def states_kernel(
    first, chunk, part, scale, index_ref, dirs_ref, weight_ref, mask_ref, freq_ref, pos_ref,
    qt_ref, kt_ref, v_ref, g_ref, *refs,
):
    kept_ref, sent_ref, cos_ref, sin_ref, k_even, q_even, k_odd, q_odd, totals, slots = refs[-10:]
    step = pl.program_id(0)
    steps = pl.num_programs(0)
    atoms = pos_ref.shape[1]
    core, pair, quad = place_of(index_ref[0])
    freq = column(freq_ref[...]) * (1.0 / (2.0 * math.pi))

    def rotate(which, bufs, start):
        for at in range(start, start + chunk, part):
            cols = slice(at, at + part)
            for j in range(2):
                i = 2 * which + j
                u = (first + step) * GROUP + i
                proj = (
                    dirs_ref[0, u] * pos_ref[0:1, cols]
                    + dirs_ref[1, u] * pos_ref[1:2, cols]
                    + dirs_ref[2, u] * pos_ref[2:3, cols]
                )
                cosine, sine = cos_sin_turns(freq * proj)
                cos_ref[i * QUARTER : (i + 1) * QUARTER, cols] = cosine.astype(BF16)
                sin_ref[i * QUARTER : (i + 1) * QUARTER, cols] = sine.astype(BF16)
                for src, dst in zip((kt_ref, qt_ref), bufs):
                    for m in range(2):
                        lead = src[QUARTER * m : QUARTER * (m + 1), cols].astype(F32)
                        trail = src[QUARTER * (m + 2) : QUARTER * (m + 3), cols].astype(F32)
                        row = j * LANES + QUARTER * m
                        dst[row : row + QUARTER, cols] = (lead * cosine - trail * sine).astype(BF16)
                        row = row + 2 * QUARTER
                        dst[row : row + QUARTER, cols] = (lead * sine + trail * cosine).astype(BF16)

    def multiply(bufs, start):
        cols = slice(start, start + chunk)
        for kind, (rot, other) in enumerate(zip(bufs, (v_ref, g_ref))):
            term = jnp.dot(rot[:, cols], other[cols, :], preferred_element_type=F32)
            totals[kind] = term if start == 0 else totals[kind] + term

    def write(which, at_step):
        for j in range(2):
            u = (first + at_step) * GROUP + 2 * which + j
            coef = weight_ref[u] * mask_ref[u].astype(F32) * scale
            rows = pl.ds(pl.multiple_of(at_step * 2 * QUARTER + j * QUARTER, QUARTER), QUARTER)
            for kind in range(2):
                for m in range(QUADS):
                    row = j * LANES + m * QUARTER
                    slots[kind ^ core, which ^ pair, slot_of(m, quad), rows, :] = (
                        totals[kind, row : row + QUARTER, :] * coef
                    ).astype(BF16)

    even, odd = (k_even, q_even), (k_odd, q_odd)
    for which, now, before in ((0, even, odd), (1, odd, even)):
        for start in range(0, atoms, chunk):
            multiply(before, start)
            rotate(which, now, start)
        write(1 - which, step if which == 1 else jnp.maximum(step - 1, 0))

    @pl.when(step == steps - 1)
    def _():
        for start in range(0, atoms, chunk):
            multiply(odd, start)
        write(1, step)
        kept_ref[...] = slots[0]
        sent_ref[...] = slots[1]


def rotated(x, cosine, sine):
    pieces = []
    for i in range(GROUP):
        c = cosine[i * QUARTER : (i + 1) * QUARTER]
        s = sine[i * QUARTER : (i + 1) * QUARTER]
        quarters = [x[m * QUARTER : (m + 1) * QUARTER] for m in range(QUADS)]
        pieces += [quarters[m] * c - quarters[m + 2] * s for m in range(2)]
        pieces += [quarters[m] * s + quarters[m + 2] * c for m in range(2)]
    return jnp.concatenate(pieces, axis=0)


def mix_kernel(chunks, part, index_ref, half_ref, *refs):
    del half_ref
    sources, refs = refs[: 4 * len(chunks)], refs[4 * len(chunks) :]
    vt_ref, gt_ref, kt_ref, qt_ref, cos_ref, sin_ref, gain_ref, out_ref = refs[:8]
    slots, states, states_t, *totals = refs[8:]
    group = pl.program_id(0)
    core, pair, quad = place_of(index_ref[0])

    @pl.when(group == 0)
    def _():
        done = 0
        for at, groups in enumerate(chunks):
            rows = groups * 2 * QUARTER
            for place, source in enumerate(sources[4 * at : 4 * at + 4]):
                for slot in range(QUADS):
                    slots[place // 2, place % 2, slot, done : done + rows, :] = source[
                        slot * rows : (slot + 1) * rows, :
                    ]
            done += rows
        for total in totals:
            total[...] = jnp.zeros_like(total)

    for kind in range(2):
        for i in range(GROUP):
            rows = pl.ds(
                pl.multiple_of(group * 2 * QUARTER + i % 2 * QUARTER, QUARTER), QUARTER
            )
            whole = jnp.concatenate(
                [
                    slots[kind ^ core, (i // 2) ^ pair, slot_of(m, quad), rows, :]
                    for m in range(QUADS)
                ],
                axis=0,
            )
            states[kind, i * LANES : (i + 1) * LANES, :] = whole
            states_t[kind, :, i * LANES : (i + 1) * LANES] = whole.astype(F32).T.astype(BF16)

    starts = list(range(0, vt_ref.shape[1], part))

    def backs(start):
        cols = slice(start, start + part)
        return [
            jnp.dot(states[kind], fixed[:, cols], preferred_element_type=F32)
            for kind, fixed in ((0, gt_ref), (1, vt_ref))
        ]

    def turn(start):
        cols = slice(start, start + part)
        return [
            rotated(x_ref[:, cols], cos_ref[:, cols], sin_ref[:, cols]) for x_ref in (qt_ref, kt_ref)
        ]

    back, turned = backs(starts[0]), turn(starts[0])
    for at, start in enumerate(starts):
        cols = slice(start, start + part)
        for kind, direct in ((0, totals[0]), (1, totals[3])):
            direct[:, cols] += jnp.dot(
                states_t[kind], turned[kind], preferred_element_type=F32
            )
        if start != starts[-1]:
            next_back = backs(starts[at + 1])
        cosine = cos_ref[:, cols].astype(F32)
        sine = sin_ref[:, cols].astype(F32)
        for kind, total in ((0, totals[1]), (1, totals[2])):
            for m in range(2):
                lead_rows = slice(QUARTER * m, QUARTER * (m + 1))
                trail_rows = slice(QUARTER * (m + 2), QUARTER * (m + 3))
                lead_total = total[lead_rows, cols]
                trail_total = total[trail_rows, cols]
                for i in range(GROUP):
                    c = cosine[i * QUARTER : (i + 1) * QUARTER]
                    s = sine[i * QUARTER : (i + 1) * QUARTER]
                    row = i * LANES + QUARTER * m
                    lead = back[kind][row : row + QUARTER, :]
                    trail = back[kind][row + 2 * QUARTER : row + 3 * QUARTER, :]
                    lead_total = lead_total + (lead * c + trail * s)
                    trail_total = trail_total + (trail * c - lead * s)
                total[lead_rows, cols] = lead_total
                total[trail_rows, cols] = trail_total
        if start != starts[-1]:
            back, turned = next_back, turn(starts[at + 1])

    @pl.when(group == pl.num_programs(0) - 1)
    def _():
        for at, total in enumerate(totals):
            whole = total[...] * gain_ref[...] if at == 2 else total[...]
            out_ref[:, at * LANES : (at + 1) * LANES] = whole.T.astype(out_ref.dtype)


def added(*terms):
    return sum(term.astype(F32) for term in terms).astype(BF16)


def per_device(
    atom_devices, queries, keys, values, cotangent, positions, species, domain, species_gain,
    frequency, directions, dir_weight, dir_mask,
):
    atoms, feats = queries.shape
    total_groups = dir_weight.shape[0] // GROUP
    half_atoms = atoms // 2
    index = lax.axis_index("atoms")[None].astype(jnp.int32)
    mine = lax.axis_index("dirs").astype(jnp.int32)
    vmem = pl.BlockSpec(memory_space=pltpu.VMEM)
    smem = pl.BlockSpec(memory_space=pltpu.SMEM)
    anywhere = pl.BlockSpec(memory_space=pl.ANY)
    params = pltpu.CompilerParams(vmem_limit_bytes=VMEM_LIMIT)
    shape = jax.ShapeDtypeStruct

    qt, kt, vt, gt, gain = pl.pallas_call(
        prepare_kernel,
        in_specs=[smem] + [vmem] * 7,
        out_specs=[vmem] * 5,
        out_shape=[shape((feats, atoms), BF16)] * 4 + [shape((feats, atoms), F32)],
        compiler_params=params,
        name="prepare",
    )(index, domain[None, :], species[None, :], species_gain, queries, keys, values, cotangent)

    def make_states(first, groups, after, phases):
        sent = shape((2, QUADS, groups * 2 * QUARTER, feats), BF16)
        phase = shape((total_groups * GROUP * QUARTER, atoms), BF16)
        phase_spec = pl.BlockSpec((GROUP * QUARTER, atoms), lambda g: (g + first, 0))
        operands = [
            index, directions, dir_weight, dir_mask, frequency[None, :], positions, qt, kt,
            values, cotangent, *after,
        ]
        kept, sent, *phases = pl.pallas_call(
            functools.partial(
                states_kernel, first, min(512, atoms), min(256, atoms),
                1.0 / math.sqrt(feats * atoms),
            ),
            grid=(groups,),
            in_specs=[smem] * 4 + [vmem] * 6 + [anywhere] * (len(after) + len(phases)),
            out_specs=[vmem] * 2 + [phase_spec] * 2,
            out_shape=[sent] * 2 + [phase] * 2,
            input_output_aliases={len(operands) + at: 2 + at for at in range(len(phases))},
            scratch_shapes=[pltpu.VMEM((2 * LANES, atoms), BF16)] * 4
            + [
                pltpu.VMEM((2, 2 * LANES, feats), F32),
                pltpu.VMEM((2, *sent.shape), BF16),
            ],
            compiler_params=params,
            cost_estimate=pl.CostEstimate(
                flops=8 * groups * WIDTH * atoms * feats,
                bytes_accessed=2 * groups * WIDTH * atoms, transcendentals=0,
            ),
            name="states",
        )(*operands, *phases)
        return kept, sent, phases

    def moved(x, target):
        return lax.ppermute(x, "atoms", [(i, target(i)) for i in range(atom_devices)])

    def by_bit(x, bit):
        return moved(x, lambda i: i ^ bit)

    def crossing(kept, sent):
        arrived = by_bit(sent, 1)
        return arrived, added(kept[1], arrived[1])

    def summed(kept, arrived, crossing_out):
        half = added(kept[0], arrived[0], by_bit(crossing_out, 2))
        near = added(half[:2], by_bit(half[2:], 4))
        quarter = added(near[0], by_bit(near[1], 8))
        whole = quarter
        for step in range(16, atom_devices, 16):
            whole = added(whole, moved(quarter, lambda i: (i + step) % atom_devices))
        near = jnp.concatenate([whole, by_bit(whole, 8)], axis=0)
        half = jnp.concatenate([near, by_bit(near, 4)], axis=0)
        other = by_bit(half, 2)
        return half, other, by_bit(half, 1), by_bit(other, 1)

    def mix(half, pieces, phases, dtype, after=()):
        rows_half = pl.BlockSpec((feats, half_atoms), lambda g, index, half: (0, half[0]))
        phase_spec = pl.BlockSpec(
            (GROUP * QUARTER, half_atoms), lambda g, index, half: (g, half[0])
        )
        return pl.pallas_call(
            lambda *refs: mix_kernel(
                CHUNKS, min(256, half_atoms), *refs[: 2 + len(pieces) + 7],
                *refs[2 + len(pieces) + 7 + len(after) :],
            ),
            grid_spec=pltpu.PrefetchScalarGridSpec(
                num_scalar_prefetch=2,
                grid=(total_groups,),
                in_specs=[vmem] * len(pieces) + [rows_half] * 4 + [phase_spec] * 2 + [rows_half]
                + [anywhere] * len(after),
                out_specs=pl.BlockSpec((half_atoms, 4 * feats), lambda g, index, half: (0, 0)),
                scratch_shapes=[
                    pltpu.VMEM((2, 2, QUADS, total_groups * 2 * QUARTER, feats), BF16),
                    pltpu.VMEM((2, WIDTH, feats), BF16),
                    pltpu.VMEM((2, feats, WIDTH), BF16),
                ]
                + [pltpu.VMEM((feats, half_atoms), F32)] * 4,
            ),
            out_shape=shape((half_atoms, 4 * feats), dtype),
            compiler_params=params,
            cost_estimate=pl.CostEstimate(
                flops=8 * total_groups * WIDTH * half_atoms * feats,
                bytes_accessed=2 * total_groups * WIDTH * half_atoms, transcendentals=0,
            ),
            name="mix",
        )(index, half[None], *pieces, vt, gt, kt, qt, *phases, gain, *after)

    made = []
    first = 0
    phases = []
    for groups in CHUNKS:
        after = [made[-2][2]] if len(made) > 1 else []
        kept, sent, phases = make_states(first, groups, after, phases)
        made.append((kept, *crossing(kept, sent)))
        first += groups
    pieces = [piece for each in made for piece in summed(*each)]
    sent = mix(1 - mine, pieces, phases, BF16)
    theirs = lax.ppermute(sent, "dirs", [(0, 1), (1, 0)])
    ours = mix(mine, pieces, phases, F32, [sent])
    total = (ours + theirs.astype(F32)).astype(BF16)
    return tuple(total[:, at * feats : (at + 1) * feats] for at in range(4))


def solution(mesh):
    return jax.shard_map(
        functools.partial(per_device, mesh.shape["atoms"]),
        mesh=mesh,
        in_specs=(
            P("atoms", None),
            P("atoms", None),
            P("atoms", None),
            P("atoms", None),
            P(None, "atoms"),
            P("atoms"),
            P("atoms"),
            P(),
            P(),
            P(None, "dirs"),
            P("dirs"),
            P("dirs"),
        ),
        out_specs=(
            P(("atoms", "dirs"), None),
            P(("atoms", "dirs"), None),
            P(("atoms", "dirs"), None),
            P(("atoms", "dirs"), None),
        ),
        check_vma=False,
    )
```

```python
import functools
import math

import jax
import jax.numpy as jnp
from jax import lax
from jax.experimental import pallas as pl
from jax.experimental.pallas import tpu as pltpu
from jax.sharding import PartitionSpec as P

BF16 = jnp.bfloat16
F32 = jnp.float32
GROUP = 4
QUADS = 4
LANES = 128
QUARTER = LANES // QUADS
WIDTH = GROUP * LANES
VMEM_LIMIT = 56 * 2**20
CHUNKS = (4, 4, 3)

SIN_COEF = (4.4428679, -7.30744342, 3.59478808, -0.78437403)
COS_COEF = (1.41420408, -6.97764206, 5.71523839, -1.72834866)


def cos_sin_turns(turns):
    part = turns - jnp.round(turns)
    square = part * part
    sine = SIN_COEF[2] + square * SIN_COEF[3]
    sine = SIN_COEF[1] + square * sine
    sine = part * (SIN_COEF[0] + square * sine)
    cosine = COS_COEF[2] + square * COS_COEF[3]
    cosine = COS_COEF[1] + square * cosine
    cosine = COS_COEF[0] + square * cosine
    return 1.0 - sine * sine, sine * cosine


def column(row):
    size = row.shape[1]
    at_row = lax.broadcasted_iota(jnp.int32, (size, size), 0)
    at_lane = lax.broadcasted_iota(jnp.int32, (size, size), 1)
    return jnp.sum(jnp.where(at_row == at_lane, row, 0.0), axis=1, keepdims=True)


def place_of(index):
    return index & 1, (index >> 1) & 1, (index >> 2) & 3


def slot_of(block, quad):
    away = block ^ quad
    return ((away & 1) << 1) | (away >> 1)


def prepare_kernel(
    index_ref, domain_ref, species_ref, gain_ref, q_ref, k_ref, v_ref, g_ref,
    qt_ref, kt_ref, vt_ref, gt_ref, gain_out,
):
    alive = (domain_ref[...] == index_ref[0]).astype(F32)
    species = species_ref[...]
    gain = jnp.zeros(gain_out.shape, F32)
    for s in range(gain_ref.shape[0]):
        gain = jnp.where(species == s, column(gain_ref[s : s + 1, :]), gain)
    gain_out[...] = gain
    kt_ref[...] = (k_ref[...].astype(F32).T * gain * alive).astype(BF16)
    qt_ref[...] = (q_ref[...].astype(F32).T * alive).astype(BF16)
    vt_ref[...] = (v_ref[...].astype(F32).T * alive).astype(BF16)
    gt_ref[...] = (g_ref[...].astype(F32).T * alive).astype(BF16)


def states_kernel(
    first, part, scale, index_ref, dirs_ref, weight_ref, mask_ref, freq_ref, pos_ref,
    qt_ref, kt_ref, v_ref, g_ref, *refs,
):
    kept_ref, sent_ref, cos_ref, sin_ref, kr, qr, slots = refs[-7:]
    group = first + pl.program_id(0)
    core, pair, quad = place_of(index_ref[0])
    freq = column(freq_ref[...]) * (1.0 / (2.0 * math.pi))
    for start in range(0, pos_ref.shape[1], part):
        cols = slice(start, start + part)
        cosines, sines = [], []
        for i in range(GROUP):
            u = group * GROUP + i
            proj = (
                dirs_ref[0, u] * pos_ref[0:1, cols]
                + dirs_ref[1, u] * pos_ref[1:2, cols]
                + dirs_ref[2, u] * pos_ref[2:3, cols]
            )
            cosine, sine = cos_sin_turns(freq * proj)
            cosines.append(cosine.astype(BF16))
            sines.append(sine.astype(BF16))
        cosine = jnp.concatenate(cosines, axis=0)
        sine = jnp.concatenate(sines, axis=0)
        cos_ref[:, cols] = cosine
        sin_ref[:, cols] = sine
        kr[:, cols] = rotated(kt_ref[:, cols], cosine, sine)
        qr[:, cols] = rotated(qt_ref[:, cols], cosine, sine)

    for kind, rot, other in ((0, kr, v_ref), (1, qr, g_ref)):
        total = jnp.dot(rot[...], other[...], preferred_element_type=F32)
        for i in range(GROUP):
            u = group * GROUP + i
            coef = weight_ref[u] * mask_ref[u].astype(F32) * scale
            rows = slice(i % 2 * QUARTER, (i % 2 + 1) * QUARTER)
            for m in range(QUADS):
                row = i * LANES + m * QUARTER
                slots[kind ^ core, (i // 2) ^ pair, slot_of(m, quad), rows, :] = (
                    total[row : row + QUARTER, :] * coef
                ).astype(BF16)
    kept_ref[...] = slots[0]
    sent_ref[...] = slots[1]


def rotated(x, cosine, sine):
    pieces = []
    for i in range(GROUP):
        c = cosine[i * QUARTER : (i + 1) * QUARTER]
        s = sine[i * QUARTER : (i + 1) * QUARTER]
        quarters = [x[m * QUARTER : (m + 1) * QUARTER] for m in range(QUADS)]
        pieces += [quarters[m] * c - quarters[m + 2] * s for m in range(2)]
        pieces += [quarters[m] * s + quarters[m + 2] * c for m in range(2)]
    return jnp.concatenate(pieces, axis=0)


def mix_kernel(chunks, part, index_ref, half_ref, *refs):
    del half_ref
    sources, refs = refs[: 4 * len(chunks)], refs[4 * len(chunks) :]
    vt_ref, gt_ref, kt_ref, qt_ref, cos_ref, sin_ref, gain_ref, out_ref = refs[:8]
    slots, states, states_t, *totals = refs[8:]
    group = pl.program_id(0)
    core, pair, quad = place_of(index_ref[0])

    @pl.when(group == 0)
    def _():
        done = 0
        for at, groups in enumerate(chunks):
            rows = groups * 2 * QUARTER
            for place, source in enumerate(sources[4 * at : 4 * at + 4]):
                for slot in range(QUADS):
                    slots[place // 2, place % 2, slot, done : done + rows, :] = source[
                        slot * rows : (slot + 1) * rows, :
                    ]
            done += rows
        for total in totals:
            total[...] = jnp.zeros_like(total)

    for kind in range(2):
        for i in range(GROUP):
            rows = pl.ds(
                pl.multiple_of(group * 2 * QUARTER + i % 2 * QUARTER, QUARTER), QUARTER
            )
            whole = jnp.concatenate(
                [
                    slots[kind ^ core, (i // 2) ^ pair, slot_of(m, quad), rows, :]
                    for m in range(QUADS)
                ],
                axis=0,
            )
            states[kind, i * LANES : (i + 1) * LANES, :] = whole
            states_t[kind, :, i * LANES : (i + 1) * LANES] = whole.astype(F32).T.astype(BF16)

    starts = list(range(0, vt_ref.shape[1], part))

    def backs(start):
        cols = slice(start, start + part)
        return [
            jnp.dot(states[kind], fixed[:, cols], preferred_element_type=F32)
            for kind, fixed in ((0, gt_ref), (1, vt_ref))
        ]

    def turn(start):
        cols = slice(start, start + part)
        return [
            rotated(x_ref[:, cols], cos_ref[:, cols], sin_ref[:, cols]) for x_ref in (qt_ref, kt_ref)
        ]

    back, turned = backs(starts[0]), turn(starts[0])
    for at, start in enumerate(starts):
        cols = slice(start, start + part)
        for kind, direct in ((0, totals[0]), (1, totals[3])):
            direct[:, cols] += jnp.dot(
                states_t[kind], turned[kind], preferred_element_type=F32
            )
        if start != starts[-1]:
            next_back = backs(starts[at + 1])
        cosine = cos_ref[:, cols].astype(F32)
        sine = sin_ref[:, cols].astype(F32)
        for kind, total in ((0, totals[1]), (1, totals[2])):
            for m in range(2):
                lead_rows = slice(QUARTER * m, QUARTER * (m + 1))
                trail_rows = slice(QUARTER * (m + 2), QUARTER * (m + 3))
                lead_total = total[lead_rows, cols]
                trail_total = total[trail_rows, cols]
                for i in range(GROUP):
                    c = cosine[i * QUARTER : (i + 1) * QUARTER]
                    s = sine[i * QUARTER : (i + 1) * QUARTER]
                    row = i * LANES + QUARTER * m
                    lead = back[kind][row : row + QUARTER, :]
                    trail = back[kind][row + 2 * QUARTER : row + 3 * QUARTER, :]
                    lead_total = lead_total + (lead * c + trail * s)
                    trail_total = trail_total + (trail * c - lead * s)
                total[lead_rows, cols] = lead_total
                total[trail_rows, cols] = trail_total
        if start != starts[-1]:
            back, turned = next_back, turn(starts[at + 1])

    @pl.when(group == pl.num_programs(0) - 1)
    def _():
        for at, total in enumerate(totals):
            whole = total[...] * gain_ref[...] if at == 2 else total[...]
            out_ref[:, at * LANES : (at + 1) * LANES] = whole.T.astype(out_ref.dtype)


def added(*terms):
    return sum(term.astype(F32) for term in terms).astype(BF16)


def per_device(
    atom_devices, queries, keys, values, cotangent, positions, species, domain, species_gain,
    frequency, directions, dir_weight, dir_mask,
):
    atoms, feats = queries.shape
    total_groups = dir_weight.shape[0] // GROUP
    half_atoms = atoms // 2
    index = lax.axis_index("atoms")[None].astype(jnp.int32)
    mine = lax.axis_index("dirs").astype(jnp.int32)
    vmem = pl.BlockSpec(memory_space=pltpu.VMEM)
    smem = pl.BlockSpec(memory_space=pltpu.SMEM)
    anywhere = pl.BlockSpec(memory_space=pl.ANY)
    params = pltpu.CompilerParams(vmem_limit_bytes=VMEM_LIMIT)
    shape = jax.ShapeDtypeStruct

    qt, kt, vt, gt, gain = pl.pallas_call(
        prepare_kernel,
        in_specs=[smem] + [vmem] * 7,
        out_specs=[vmem] * 5,
        out_shape=[shape((feats, atoms), BF16)] * 4 + [shape((feats, atoms), F32)],
        compiler_params=params,
        name="prepare",
    )(index, domain[None, :], species[None, :], species_gain, queries, keys, values, cotangent)

    def make_states(first, groups, after, phases):
        sent = shape((2, QUADS, groups * 2 * QUARTER, feats), BF16)
        sent_spec = pl.BlockSpec((2, QUADS, 2 * QUARTER, feats), lambda g: (0, 0, g, 0))
        phase = shape((total_groups * GROUP * QUARTER, atoms), BF16)
        phase_spec = pl.BlockSpec((GROUP * QUARTER, atoms), lambda g: (g + first, 0))
        operands = [
            index, directions, dir_weight, dir_mask, frequency[None, :], positions, qt, kt,
            values, cotangent, *after,
        ]
        kept, sent, *phases = pl.pallas_call(
            functools.partial(states_kernel, first, min(256, atoms), 1.0 / math.sqrt(feats * atoms)),
            grid=(groups,),
            in_specs=[smem] * 4 + [vmem] * 6 + [anywhere] * (len(after) + len(phases)),
            out_specs=[sent_spec] * 2 + [phase_spec] * 2,
            out_shape=[sent] * 2 + [phase] * 2,
            input_output_aliases={len(operands) + at: 2 + at for at in range(len(phases))},
            scratch_shapes=[pltpu.VMEM((WIDTH, atoms), BF16)] * 2
            + [pltpu.VMEM((2, 2, QUADS, 2 * QUARTER, feats), BF16)],
            compiler_params=params,
            cost_estimate=pl.CostEstimate(
                flops=8 * groups * WIDTH * atoms * feats,
                bytes_accessed=2 * groups * WIDTH * atoms, transcendentals=0,
            ),
            name="states",
        )(*operands, *phases)
        return kept, sent, phases

    def moved(x, target):
        return lax.ppermute(x, "atoms", [(i, target(i)) for i in range(atom_devices)])

    def by_bit(x, bit):
        return moved(x, lambda i: i ^ bit)

    def crossing(kept, sent):
        arrived = by_bit(sent, 1)
        return arrived, added(kept[1], arrived[1])

    def summed(kept, arrived, crossing_out):
        half = added(kept[0], arrived[0], by_bit(crossing_out, 2))
        near = added(half[:2], by_bit(half[2:], 4))
        near = added(near, by_bit(near, 8)[::-1])
        total = near
        for step in range(16, atom_devices, 16):
            total = added(total, moved(near, lambda i: (i + step) % atom_devices))
        near = total.reshape(-1, feats)
        half = jnp.concatenate([near, by_bit(near, 4)], axis=0)
        other = by_bit(half, 2)
        return half, other, by_bit(half, 1), by_bit(other, 1)

    def mix(half, pieces, phases, dtype, after=()):
        rows_half = pl.BlockSpec((feats, half_atoms), lambda g, index, half: (0, half[0]))
        phase_spec = pl.BlockSpec(
            (GROUP * QUARTER, half_atoms), lambda g, index, half: (g, half[0])
        )
        return pl.pallas_call(
            lambda *refs: mix_kernel(
                CHUNKS, min(256, half_atoms), *refs[: 2 + len(pieces) + 7],
                *refs[2 + len(pieces) + 7 + len(after) :],
            ),
            grid_spec=pltpu.PrefetchScalarGridSpec(
                num_scalar_prefetch=2,
                grid=(total_groups,),
                in_specs=[vmem] * len(pieces) + [rows_half] * 4 + [phase_spec] * 2 + [rows_half]
                + [anywhere] * len(after),
                out_specs=pl.BlockSpec((half_atoms, 4 * feats), lambda g, index, half: (0, 0)),
                scratch_shapes=[
                    pltpu.VMEM((2, 2, QUADS, total_groups * 2 * QUARTER, feats), BF16),
                    pltpu.VMEM((2, WIDTH, feats), BF16),
                    pltpu.VMEM((2, feats, WIDTH), BF16),
                ]
                + [pltpu.VMEM((feats, half_atoms), F32)] * 4,
            ),
            out_shape=shape((half_atoms, 4 * feats), dtype),
            compiler_params=params,
            cost_estimate=pl.CostEstimate(
                flops=8 * total_groups * WIDTH * half_atoms * feats,
                bytes_accessed=2 * total_groups * WIDTH * half_atoms, transcendentals=0,
            ),
            name="mix",
        )(index, half[None], *pieces, vt, gt, kt, qt, *phases, gain, *after)

    made = []
    first = 0
    phases = []
    for groups in CHUNKS:
        after = [made[-2][2]] if len(made) > 1 else []
        kept, sent, phases = make_states(first, groups, after, phases)
        made.append((kept, *crossing(kept, sent)))
        first += groups
    pieces = [piece for each in made for piece in summed(*each)]
    sent = mix(1 - mine, pieces, phases, BF16)
    theirs = lax.ppermute(sent, "dirs", [(0, 1), (1, 0)])
    ours = mix(mine, pieces, phases, F32, [sent])
    lanes = [slice(at * feats, (at + 1) * feats) for at in range(4)]
    return tuple((ours[:, at] + theirs[:, at].astype(F32)).astype(BF16) for at in lanes)


def solution(mesh):
    return jax.shard_map(
        functools.partial(per_device, mesh.shape["atoms"]),
        mesh=mesh,
        in_specs=(
            P("atoms", None),
            P("atoms", None),
            P("atoms", None),
            P("atoms", None),
            P(None, "atoms"),
            P("atoms"),
            P("atoms"),
            P(),
            P(),
            P(None, "dirs"),
            P("dirs"),
            P("dirs"),
        ),
        out_specs=(
            P(("atoms", "dirs"), None),
            P(("atoms", "dirs"), None),
            P(("atoms", "dirs"), None),
            P(("atoms", "dirs"), None),
        ),
        check_vma=False,
    )
```

```python
import functools
import math

import jax
import jax.numpy as jnp
from jax import lax
from jax.experimental import pallas as pl
from jax.experimental.pallas import tpu as pltpu
from jax.sharding import PartitionSpec as P

BF16 = jnp.bfloat16
F32 = jnp.float32
GROUP = 4
QUADS = 4
LANES = 128
QUARTER = LANES // QUADS
WIDTH = GROUP * LANES
VMEM_LIMIT = 56 * 2**20
CHUNKS = (5, 4, 2)

SIN_COEF = (4.4428679, -7.30744342, 3.59478808, -0.78437403)
COS_COEF = (1.41420408, -6.97764206, 5.71523839, -1.72834866)


def cos_sin_turns(turns):
    part = turns - jnp.round(turns)
    square = part * part
    sine = SIN_COEF[2] + square * SIN_COEF[3]
    sine = SIN_COEF[1] + square * sine
    sine = part * (SIN_COEF[0] + square * sine)
    cosine = COS_COEF[2] + square * COS_COEF[3]
    cosine = COS_COEF[1] + square * cosine
    cosine = COS_COEF[0] + square * cosine
    return 1.0 - sine * sine, sine * cosine


def column(row):
    size = row.shape[1]
    at_row = lax.broadcasted_iota(jnp.int32, (size, size), 0)
    at_lane = lax.broadcasted_iota(jnp.int32, (size, size), 1)
    return jnp.sum(jnp.where(at_row == at_lane, row, 0.0), axis=1, keepdims=True)


def place_of(index):
    return index & 1, (index >> 1) & 1, (index >> 2) & 3


def slot_of(block, quad):
    away = block ^ quad
    return ((away & 1) << 1) | (away >> 1)


def prepare_kernel(
    index_ref, domain_ref, species_ref, gain_ref, q_ref, k_ref, v_ref, g_ref,
    qt_ref, kt_ref, vt_ref, gt_ref, gain_out,
):
    alive = (domain_ref[...] == index_ref[0]).astype(F32)
    species = species_ref[...]
    gain = jnp.zeros(gain_out.shape, F32)
    for s in range(gain_ref.shape[0]):
        gain = jnp.where(species == s, column(gain_ref[s : s + 1, :]), gain)
    gain_out[...] = gain
    kt_ref[...] = (k_ref[...].astype(F32).T * gain * alive).astype(BF16)
    qt_ref[...] = (q_ref[...].astype(F32).T * alive).astype(BF16)
    vt_ref[...] = (v_ref[...].astype(F32).T * alive).astype(BF16)
    gt_ref[...] = (g_ref[...].astype(F32).T * alive).astype(BF16)


def states_kernel(
    first, part, scale, index_ref, dirs_ref, weight_ref, mask_ref, freq_ref, pos_ref,
    qt_ref, kt_ref, v_ref, g_ref, *refs,
):
    kept_ref, sent_ref, cos_ref, sin_ref, kr, qr, slots = refs[-7:]
    group = first + pl.program_id(0)
    core, pair, quad = place_of(index_ref[0])
    freq = column(freq_ref[...]) * (1.0 / (2.0 * math.pi))
    for start in range(0, pos_ref.shape[1], part):
        cols = slice(start, start + part)
        cosines, sines = [], []
        for i in range(GROUP):
            u = group * GROUP + i
            proj = (
                dirs_ref[0, u] * pos_ref[0:1, cols]
                + dirs_ref[1, u] * pos_ref[1:2, cols]
                + dirs_ref[2, u] * pos_ref[2:3, cols]
            )
            cosine, sine = cos_sin_turns(freq * proj)
            cosines.append(cosine.astype(BF16))
            sines.append(sine.astype(BF16))
        cosine = jnp.concatenate(cosines, axis=0)
        sine = jnp.concatenate(sines, axis=0)
        cos_ref[:, cols] = cosine
        sin_ref[:, cols] = sine
        kr[:, cols] = rotated(kt_ref[:, cols], cosine, sine)
        qr[:, cols] = rotated(qt_ref[:, cols], cosine, sine)

    for kind, rot, other in ((0, kr, v_ref), (1, qr, g_ref)):
        total = jnp.dot(rot[...], other[...], preferred_element_type=F32)
        for i in range(GROUP):
            u = group * GROUP + i
            coef = weight_ref[u] * mask_ref[u].astype(F32) * scale
            rows = slice(i % 2 * QUARTER, (i % 2 + 1) * QUARTER)
            for m in range(QUADS):
                row = i * LANES + m * QUARTER
                slots[kind ^ core, (i // 2) ^ pair, slot_of(m, quad), rows, :] = (
                    total[row : row + QUARTER, :] * coef
                ).astype(BF16)
    kept_ref[...] = slots[0]
    sent_ref[...] = slots[1]


def rotated(x, cosine, sine):
    pieces = []
    for i in range(GROUP):
        c = cosine[i * QUARTER : (i + 1) * QUARTER]
        s = sine[i * QUARTER : (i + 1) * QUARTER]
        quarters = [x[m * QUARTER : (m + 1) * QUARTER] for m in range(QUADS)]
        pieces += [quarters[m] * c - quarters[m + 2] * s for m in range(2)]
        pieces += [quarters[m] * s + quarters[m + 2] * c for m in range(2)]
    return jnp.concatenate(pieces, axis=0)


def mix_kernel(chunks, part, index_ref, half_ref, *refs):
    del half_ref
    sources, refs = refs[: 4 * len(chunks)], refs[4 * len(chunks) :]
    vt_ref, gt_ref, kt_ref, qt_ref, cos_ref, sin_ref, gain_ref, out_ref = refs[:8]
    slots, states, states_t, *totals = refs[8:]
    group = pl.program_id(0)
    core, pair, quad = place_of(index_ref[0])

    @pl.when(group == 0)
    def _():
        done = 0
        for at, groups in enumerate(chunks):
            rows = groups * 2 * QUARTER
            for place, source in enumerate(sources[4 * at : 4 * at + 4]):
                for slot in range(QUADS):
                    slots[place // 2, place % 2, slot, done : done + rows, :] = source[
                        slot * rows : (slot + 1) * rows, :
                    ]
            done += rows
        for total in totals:
            total[...] = jnp.zeros_like(total)

    for kind in range(2):
        for i in range(GROUP):
            rows = pl.ds(
                pl.multiple_of(group * 2 * QUARTER + i % 2 * QUARTER, QUARTER), QUARTER
            )
            whole = jnp.concatenate(
                [
                    slots[kind ^ core, (i // 2) ^ pair, slot_of(m, quad), rows, :]
                    for m in range(QUADS)
                ],
                axis=0,
            )
            states[kind, i * LANES : (i + 1) * LANES, :] = whole
            states_t[kind, :, i * LANES : (i + 1) * LANES] = whole.astype(F32).T.astype(BF16)

    starts = list(range(0, vt_ref.shape[1], part))

    def backs(start):
        cols = slice(start, start + part)
        return [
            jnp.dot(states[kind], fixed[:, cols], preferred_element_type=F32)
            for kind, fixed in ((0, gt_ref), (1, vt_ref))
        ]

    def turn(start):
        cols = slice(start, start + part)
        return [
            rotated(x_ref[:, cols], cos_ref[:, cols], sin_ref[:, cols]) for x_ref in (qt_ref, kt_ref)
        ]

    back, turned = backs(starts[0]), turn(starts[0])
    for at, start in enumerate(starts):
        cols = slice(start, start + part)
        for kind, direct in ((0, totals[0]), (1, totals[3])):
            direct[:, cols] += jnp.dot(
                states_t[kind], turned[kind], preferred_element_type=F32
            )
        if start != starts[-1]:
            next_back = backs(starts[at + 1])
        cosine = cos_ref[:, cols]
        sine = sin_ref[:, cols]
        for kind, total in ((0, totals[1]), (1, totals[2])):
            lower = back[kind].astype(BF16)
            for m in range(2):
                leads, trails = [], []
                for i in range(GROUP):
                    c = cosine[i * QUARTER : (i + 1) * QUARTER]
                    s = sine[i * QUARTER : (i + 1) * QUARTER]
                    row = i * LANES + QUARTER * m
                    lead = lower[row : row + QUARTER, :]
                    trail = lower[row + 2 * QUARTER : row + 3 * QUARTER, :]
                    leads.append(lead * c + trail * s)
                    trails.append(trail * c - lead * s)
                for block, terms in ((m, leads), (m + 2, trails)):
                    rows = slice(QUARTER * block, QUARTER * (block + 1))
                    total[rows, cols] += ((terms[0] + terms[1]) + (terms[2] + terms[3])).astype(F32)
        if start != starts[-1]:
            back, turned = next_back, turn(starts[at + 1])

    @pl.when(group == pl.num_programs(0) - 1)
    def _():
        for at, total in enumerate(totals):
            whole = total[...] * gain_ref[...] if at == 2 else total[...]
            out_ref[:, at * LANES : (at + 1) * LANES] = whole.T.astype(out_ref.dtype)


def added(*terms):
    return sum(term.astype(F32) for term in terms).astype(BF16)


def per_device(
    atom_devices, queries, keys, values, cotangent, positions, species, domain, species_gain,
    frequency, directions, dir_weight, dir_mask,
):
    atoms, feats = queries.shape
    total_groups = dir_weight.shape[0] // GROUP
    half_atoms = atoms // 2
    index = lax.axis_index("atoms")[None].astype(jnp.int32)
    mine = lax.axis_index("dirs").astype(jnp.int32)
    vmem = pl.BlockSpec(memory_space=pltpu.VMEM)
    smem = pl.BlockSpec(memory_space=pltpu.SMEM)
    anywhere = pl.BlockSpec(memory_space=pl.ANY)
    params = pltpu.CompilerParams(vmem_limit_bytes=VMEM_LIMIT)
    shape = jax.ShapeDtypeStruct

    qt, kt, vt, gt, gain = pl.pallas_call(
        prepare_kernel,
        in_specs=[smem] + [vmem] * 7,
        out_specs=[vmem] * 5,
        out_shape=[shape((feats, atoms), BF16)] * 4 + [shape((feats, atoms), F32)],
        compiler_params=params,
        name="prepare",
    )(index, domain[None, :], species[None, :], species_gain, queries, keys, values, cotangent)

    def make_states(first, groups, after, phases):
        sent = shape((2, QUADS, groups * 2 * QUARTER, feats), BF16)
        sent_spec = pl.BlockSpec((2, QUADS, 2 * QUARTER, feats), lambda g: (0, 0, g, 0))
        phase = shape((total_groups * GROUP * QUARTER, atoms), BF16)
        phase_spec = pl.BlockSpec((GROUP * QUARTER, atoms), lambda g: (g + first, 0))
        operands = [
            index, directions, dir_weight, dir_mask, frequency[None, :], positions, qt, kt,
            values, cotangent, *after,
        ]
        kept, sent, *phases = pl.pallas_call(
            functools.partial(states_kernel, first, min(256, atoms), 1.0 / math.sqrt(feats * atoms)),
            grid=(groups,),
            in_specs=[smem] * 4 + [vmem] * 6 + [anywhere] * (len(after) + len(phases)),
            out_specs=[sent_spec] * 2 + [phase_spec] * 2,
            out_shape=[sent] * 2 + [phase] * 2,
            input_output_aliases={len(operands) + at: 2 + at for at in range(len(phases))},
            scratch_shapes=[pltpu.VMEM((WIDTH, atoms), BF16)] * 2
            + [pltpu.VMEM((2, 2, QUADS, 2 * QUARTER, feats), BF16)],
            compiler_params=params,
            cost_estimate=pl.CostEstimate(
                flops=8 * groups * WIDTH * atoms * feats,
                bytes_accessed=2 * groups * WIDTH * atoms, transcendentals=0,
            ),
            name="states",
        )(*operands, *phases)
        return kept, sent, phases

    def moved(x, target):
        return lax.ppermute(x, "atoms", [(i, target(i)) for i in range(atom_devices)])

    def by_bit(x, bit):
        return moved(x, lambda i: i ^ bit)

    def crossing(kept, sent):
        arrived = by_bit(sent, 1)
        return arrived, added(kept[1], arrived[1])

    def summed(kept, arrived, crossing_out):
        half = added(kept[0], arrived[0], by_bit(crossing_out, 2))
        near = added(half[:2], by_bit(half[2:], 4))
        near = added(near, by_bit(near, 8)[::-1])
        total = near
        for step in range(16, atom_devices, 16):
            total = added(total, moved(near, lambda i: (i + step) % atom_devices))
        near = total.reshape(-1, feats)
        half = jnp.concatenate([near, by_bit(near, 4)], axis=0)
        other = by_bit(half, 2)
        return half, other, by_bit(half, 1), by_bit(other, 1)

    def mix(half, pieces, phases, dtype, after=()):
        rows_half = pl.BlockSpec((feats, half_atoms), lambda g, index, half: (0, half[0]))
        phase_spec = pl.BlockSpec(
            (GROUP * QUARTER, half_atoms), lambda g, index, half: (g, half[0])
        )
        return pl.pallas_call(
            lambda *refs: mix_kernel(
                CHUNKS, min(256, half_atoms), *refs[: 2 + len(pieces) + 7],
                *refs[2 + len(pieces) + 7 + len(after) :],
            ),
            grid_spec=pltpu.PrefetchScalarGridSpec(
                num_scalar_prefetch=2,
                grid=(total_groups,),
                in_specs=[vmem] * len(pieces) + [rows_half] * 4 + [phase_spec] * 2 + [rows_half]
                + [anywhere] * len(after),
                out_specs=pl.BlockSpec((half_atoms, 4 * feats), lambda g, index, half: (0, 0)),
                scratch_shapes=[
                    pltpu.VMEM((2, 2, QUADS, total_groups * 2 * QUARTER, feats), BF16),
                    pltpu.VMEM((2, WIDTH, feats), BF16),
                    pltpu.VMEM((2, feats, WIDTH), BF16),
                ]
                + [pltpu.VMEM((feats, half_atoms), F32)] * 4,
            ),
            out_shape=shape((half_atoms, 4 * feats), dtype),
            compiler_params=params,
            cost_estimate=pl.CostEstimate(
                flops=8 * total_groups * WIDTH * half_atoms * feats,
                bytes_accessed=2 * total_groups * WIDTH * half_atoms, transcendentals=0,
            ),
            name="mix",
        )(index, half[None], *pieces, vt, gt, kt, qt, *phases, gain, *after)

    made = []
    first = 0
    phases = []
    for groups in CHUNKS:
        after = [made[-2][2]] if len(made) > 1 else []
        kept, sent, phases = make_states(first, groups, after, phases)
        made.append((kept, *crossing(kept, sent)))
        first += groups
    pieces = [piece for each in made for piece in summed(*each)]
    sent = mix(1 - mine, pieces, phases, BF16)
    theirs = lax.ppermute(sent, "dirs", [(0, 1), (1, 0)])
    ours = mix(mine, pieces, phases, F32, [sent])
    lanes = [slice(at * feats, (at + 1) * feats) for at in range(4)]
    return tuple((ours[:, at] + theirs[:, at].astype(F32)).astype(BF16) for at in lanes)


def solution(mesh):
    return jax.shard_map(
        functools.partial(per_device, mesh.shape["atoms"]),
        mesh=mesh,
        in_specs=(
            P("atoms", None),
            P("atoms", None),
            P("atoms", None),
            P("atoms", None),
            P(None, "atoms"),
            P("atoms"),
            P("atoms"),
            P(),
            P(),
            P(None, "dirs"),
            P("dirs"),
            P("dirs"),
        ),
        out_specs=(
            P(("atoms", "dirs"), None),
            P(("atoms", "dirs"), None),
            P(("atoms", "dirs"), None),
            P(("atoms", "dirs"), None),
        ),
        check_vma=False,
    )
```

```python
import functools
import math

import jax
import jax.numpy as jnp
from jax import lax
from jax.experimental import pallas as pl
from jax.experimental.pallas import tpu as pltpu
from jax.sharding import PartitionSpec as P

BF16 = jnp.bfloat16
F32 = jnp.float32
GROUP = 4
QUADS = 4
LANES = 128
QUARTER = LANES // QUADS
WIDTH = GROUP * LANES
VMEM_LIMIT = 56 * 2**20
CHUNKS = (4, 4, 3)

SIN_COEF = (4.4428679, -7.30744342, 3.59478808, -0.78437403)
COS_COEF = (1.41420408, -6.97764206, 5.71523839, -1.72834866)


def cos_sin_turns(turns):
    part = turns - jnp.round(turns)
    square = part * part
    sine = SIN_COEF[2] + square * SIN_COEF[3]
    sine = SIN_COEF[1] + square * sine
    sine = part * (SIN_COEF[0] + square * sine)
    cosine = COS_COEF[2] + square * COS_COEF[3]
    cosine = COS_COEF[1] + square * cosine
    cosine = COS_COEF[0] + square * cosine
    return 1.0 - sine * sine, sine * cosine


def column(row):
    size = row.shape[1]
    at_row = lax.broadcasted_iota(jnp.int32, (size, size), 0)
    at_lane = lax.broadcasted_iota(jnp.int32, (size, size), 1)
    return jnp.sum(jnp.where(at_row == at_lane, row, 0.0), axis=1, keepdims=True)


def place_of(index):
    return index & 1, (index >> 1) & 1, (index >> 2) & 3


def slot_of(block, quad):
    away = block ^ quad
    return ((away & 1) << 1) | (away >> 1)


def prepare_kernel(
    index_ref, domain_ref, species_ref, gain_ref, q_ref, k_ref, v_ref, g_ref,
    qt_ref, kt_ref, vt_ref, gt_ref, gain_out,
):
    alive = (domain_ref[...] == index_ref[0]).astype(F32)
    species = species_ref[...]
    gain = jnp.zeros(gain_out.shape, F32)
    for s in range(gain_ref.shape[0]):
        gain = jnp.where(species == s, column(gain_ref[s : s + 1, :]), gain)
    gain_out[...] = gain
    kt_ref[...] = (k_ref[...].astype(F32).T * gain * alive).astype(BF16)
    qt_ref[...] = (q_ref[...].astype(F32).T * alive).astype(BF16)
    vt_ref[...] = (v_ref[...].astype(F32).T * alive).astype(BF16)
    gt_ref[...] = (g_ref[...].astype(F32).T * alive).astype(BF16)


def states_kernel(
    first, part, scale, index_ref, dirs_ref, weight_ref, mask_ref, freq_ref, pos_ref,
    qt_ref, kt_ref, v_in, g_in, *refs,
):
    kept_ref, sent_ref, cos_ref, sin_ref, kr, qr, slots, v_ref, g_ref, sems = refs[-10:]
    group = first + pl.program_id(0)
    copies = [
        pltpu.make_async_copy(v_in, v_ref, sems.at[0]),
        pltpu.make_async_copy(g_in, g_ref, sems.at[1]),
    ]

    @pl.when(pl.program_id(0) == 0)
    def _():
        for copy in copies:
            copy.start()

    core, pair, quad = place_of(index_ref[0])
    freq = column(freq_ref[...]) * (1.0 / (2.0 * math.pi))
    for start in range(0, pos_ref.shape[1], part):
        cols = slice(start, start + part)
        cosines, sines = [], []
        for i in range(GROUP):
            u = group * GROUP + i
            proj = (
                dirs_ref[0, u] * pos_ref[0:1, cols]
                + dirs_ref[1, u] * pos_ref[1:2, cols]
                + dirs_ref[2, u] * pos_ref[2:3, cols]
            )
            cosine, sine = cos_sin_turns(freq * proj)
            cosines.append(cosine.astype(BF16))
            sines.append(sine.astype(BF16))
        cosine = jnp.concatenate(cosines, axis=0)
        sine = jnp.concatenate(sines, axis=0)
        cos_ref[:, cols] = cosine
        sin_ref[:, cols] = sine
        kr[:, cols] = rotated(kt_ref[:, cols], cosine, sine)
        qr[:, cols] = rotated(qt_ref[:, cols], cosine, sine)

    @pl.when(pl.program_id(0) == 0)
    def _():
        for copy in copies:
            copy.wait()

    for kind, rot, other in ((0, kr, v_ref), (1, qr, g_ref)):
        total = jnp.dot(rot[...], other[...], preferred_element_type=F32)
        for i in range(GROUP):
            u = group * GROUP + i
            coef = weight_ref[u] * mask_ref[u].astype(F32) * scale
            rows = slice(i % 2 * QUARTER, (i % 2 + 1) * QUARTER)
            for m in range(QUADS):
                row = i * LANES + m * QUARTER
                slots[kind ^ core, (i // 2) ^ pair, slot_of(m, quad), rows, :] = (
                    total[row : row + QUARTER, :] * coef
                ).astype(BF16)
    kept_ref[...] = slots[0]
    sent_ref[...] = slots[1]


def rotated(x, cosine, sine):
    pieces = []
    for i in range(GROUP):
        c = cosine[i * QUARTER : (i + 1) * QUARTER]
        s = sine[i * QUARTER : (i + 1) * QUARTER]
        quarters = [x[m * QUARTER : (m + 1) * QUARTER] for m in range(QUADS)]
        pieces += [quarters[m] * c - quarters[m + 2] * s for m in range(2)]
        pieces += [quarters[m] * s + quarters[m + 2] * c for m in range(2)]
    return jnp.concatenate(pieces, axis=0)


def mix_kernel(chunks, part, direct_too, back_too, index_ref, half_ref, *refs):
    sources, refs = refs[: 4 * len(chunks)], refs[4 * len(chunks) :]
    vt_ref, gt_ref, kt_ref, qt_ref, cos_ref, sin_ref, gain_in, out_ref = refs[:8]
    slots, states, states_t, *totals, gain_ref, sem = refs[8:]
    group = pl.program_id(0)
    atoms = gain_ref.shape[1]
    gain_copy = back_too and pltpu.make_async_copy(
        gain_in.at[:, pl.ds(pl.multiple_of(half_ref[0] * atoms, atoms), atoms)], gain_ref, sem
    )
    core, pair, quad = place_of(index_ref[0])

    @pl.when(group == 0)
    def _():
        if back_too:
            gain_copy.start()
        done = 0
        for at, groups in enumerate(chunks):
            rows = groups * 2 * QUARTER
            for place, source in enumerate(sources[4 * at : 4 * at + 4]):
                for slot in range(QUADS):
                    slots[place // 2, place % 2, slot, done : done + rows, :] = source[
                        slot * rows : (slot + 1) * rows, :
                    ]
            done += rows
        for total in totals:
            total[...] = jnp.zeros_like(total)

    for kind in range(2):
        for i in range(GROUP):
            rows = pl.ds(
                pl.multiple_of(group * 2 * QUARTER + i % 2 * QUARTER, QUARTER), QUARTER
            )
            whole = jnp.concatenate(
                [
                    slots[kind ^ core, (i // 2) ^ pair, slot_of(m, quad), rows, :]
                    for m in range(QUADS)
                ],
                axis=0,
            )
            states[kind, i * LANES : (i + 1) * LANES, :] = whole
            states_t[kind, :, i * LANES : (i + 1) * LANES] = whole.astype(F32).T.astype(BF16)

    starts = list(range(0, vt_ref.shape[1], part))

    def backs(start):
        cols = slice(start, start + part)
        return back_too and [
            jnp.dot(states[kind], fixed[:, cols], preferred_element_type=F32)
            for kind, fixed in ((0, gt_ref), (1, vt_ref))
        ]

    def turn(start):
        cols = slice(start, start + part)
        return direct_too and [
            rotated(x_ref[:, cols], cos_ref[:, cols], sin_ref[:, cols]) for x_ref in (qt_ref, kt_ref)
        ]

    back, turned = backs(starts[0]), turn(starts[0])
    for at, start in enumerate(starts):
        cols = slice(start, start + part)
        for kind, direct in ((0, totals[0]), (1, totals[3])) if direct_too else ():
            direct[:, cols] += jnp.dot(
                states_t[kind], turned[kind], preferred_element_type=F32
            )
        if start != starts[-1]:
            next_back = backs(starts[at + 1])
        cosine = cos_ref[:, cols]
        sine = sin_ref[:, cols]
        for kind, total in ((0, totals[1]), (1, totals[2])) if back_too else ():
            lower = back[kind].astype(BF16)
            for m in range(2):
                leads, trails = [], []
                for i in range(GROUP):
                    c = cosine[i * QUARTER : (i + 1) * QUARTER]
                    s = sine[i * QUARTER : (i + 1) * QUARTER]
                    row = i * LANES + QUARTER * m
                    lead = lower[row : row + QUARTER, :]
                    trail = lower[row + 2 * QUARTER : row + 3 * QUARTER, :]
                    leads.append(lead * c + trail * s)
                    trails.append(trail * c - lead * s)
                for block, terms in ((m, leads), (m + 2, trails)):
                    rows = slice(QUARTER * block, QUARTER * (block + 1))
                    total[rows, cols] += ((terms[0] + terms[1]) + (terms[2] + terms[3])).astype(F32)
        if start != starts[-1]:
            back, turned = next_back, turn(starts[at + 1])

    @pl.when(group == pl.num_programs(0) - 1)
    def _():
        if back_too:
            gain_copy.wait()
        done = 0
        for at, total in enumerate(totals):
            if back_too if at in (1, 2) else direct_too:
                whole = total[...] * gain_ref[...] if at == 2 else total[...]
                out_ref[:, done : done + LANES] = whole.T.astype(out_ref.dtype)
                done += LANES


def added(*terms):
    return sum(term.astype(F32) for term in terms).astype(BF16)


def per_device(
    atom_devices, queries, keys, values, cotangent, positions, species, domain, species_gain,
    frequency, directions, dir_weight, dir_mask,
):
    atoms, feats = queries.shape
    total_groups = dir_weight.shape[0] // GROUP
    half_atoms = atoms // 2
    index = lax.axis_index("atoms")[None].astype(jnp.int32)
    mine = lax.axis_index("dirs").astype(jnp.int32)
    vmem = pl.BlockSpec(memory_space=pltpu.VMEM)
    smem = pl.BlockSpec(memory_space=pltpu.SMEM)
    anywhere = pl.BlockSpec(memory_space=pl.ANY)
    params = pltpu.CompilerParams(vmem_limit_bytes=VMEM_LIMIT)
    shape = jax.ShapeDtypeStruct

    qt, kt, vt, gt, gain = pl.pallas_call(
        prepare_kernel,
        in_specs=[smem] + [vmem] * 7,
        out_specs=[vmem] * 5,
        out_shape=[shape((feats, atoms), BF16)] * 4 + [shape((feats, atoms), F32)],
        compiler_params=params,
        name="prepare",
    )(index, domain[None, :], species[None, :], species_gain, queries, keys, values, cotangent)

    def make_states(first, groups, after, phases):
        sent = shape((2, QUADS, groups * 2 * QUARTER, feats), BF16)
        sent_spec = pl.BlockSpec((2, QUADS, 2 * QUARTER, feats), lambda g: (0, 0, g, 0))
        phase = shape((total_groups * GROUP * QUARTER, atoms), BF16)
        phase_spec = pl.BlockSpec((GROUP * QUARTER, atoms), lambda g: (g + first, 0))
        operands = [
            index, directions, dir_weight, dir_mask, frequency[None, :], positions, qt, kt,
            values, cotangent, *after,
        ]
        kept, sent, *phases = pl.pallas_call(
            functools.partial(states_kernel, first, min(256, atoms), 1.0 / math.sqrt(feats * atoms)),
            grid=(groups,),
            in_specs=[smem] * 4 + [vmem] * 4 + [anywhere] * (2 + len(after) + len(phases)),
            out_specs=[sent_spec] * 2 + [phase_spec] * 2,
            out_shape=[sent] * 2 + [phase] * 2,
            input_output_aliases={len(operands) + at: 2 + at for at in range(len(phases))},
            scratch_shapes=[pltpu.VMEM((WIDTH, atoms), BF16)] * 2
            + [pltpu.VMEM((2, 2, QUADS, 2 * QUARTER, feats), BF16)]
            + [pltpu.VMEM((atoms, feats), BF16)] * 2
            + [pltpu.SemaphoreType.DMA((2,))],
            compiler_params=params,
            cost_estimate=pl.CostEstimate(
                flops=8 * groups * WIDTH * atoms * feats,
                bytes_accessed=2 * groups * WIDTH * atoms, transcendentals=0,
            ),
            name="states",
        )(*operands, *phases)
        return kept, sent, phases

    def moved(x, target):
        return lax.ppermute(x, "atoms", [(i, target(i)) for i in range(atom_devices)])

    def by_bit(x, bit):
        return moved(x, lambda i: i ^ bit)

    def crossing(kept, sent):
        arrived = by_bit(sent, 1)
        return arrived, added(kept[1], arrived[1])

    def summed(kept, arrived, crossing_out):
        half = added(kept[0], arrived[0], by_bit(crossing_out, 2))
        near = added(half[:2], by_bit(half[2:], 4))
        near = added(near, by_bit(near, 8)[::-1])
        total = near
        for step in range(16, atom_devices, 16):
            total = added(total, moved(near, lambda i: (i + step) % atom_devices))
        near = total.reshape(-1, feats)
        half = jnp.concatenate([near, by_bit(near, 4)], axis=0)
        other = by_bit(half, 2)
        return half, other, by_bit(half, 1), by_bit(other, 1)

    def mix(half, pieces, phases, direct_too, back_too, after=()):
        lanes = 2 * feats * (direct_too + back_too)
        rows_half = pl.BlockSpec((feats, half_atoms), lambda g, index, half: (0, half[0]))
        phase_spec = pl.BlockSpec(
            (GROUP * QUARTER, half_atoms), lambda g, index, half: (g, half[0])
        )
        return pl.pallas_call(
            lambda *refs: mix_kernel(
                CHUNKS, min(256, half_atoms), direct_too, back_too, *refs[: 2 + len(pieces) + 7],
                *refs[2 + len(pieces) + 7 + len(after) :],
            ),
            grid_spec=pltpu.PrefetchScalarGridSpec(
                num_scalar_prefetch=2,
                grid=(total_groups,),
                in_specs=[vmem] * len(pieces) + [rows_half] * 4 + [phase_spec] * 2 + [anywhere]
                + [anywhere] * len(after),
                out_specs=pl.BlockSpec((half_atoms, lanes), lambda g, index, half: (0, 0)),
                scratch_shapes=[
                    pltpu.VMEM((2, 2, QUADS, total_groups * 2 * QUARTER, feats), BF16),
                    pltpu.VMEM((2, WIDTH, feats), BF16),
                    pltpu.VMEM((2, feats, WIDTH), BF16),
                ]
                + [pltpu.VMEM((feats, half_atoms), F32)] * 5
                + [pltpu.SemaphoreType.DMA],
            ),
            out_shape=shape((half_atoms, lanes), BF16),
            compiler_params=params,
            cost_estimate=pl.CostEstimate(
                flops=8 * total_groups * WIDTH * half_atoms * feats,
                bytes_accessed=2 * total_groups * WIDTH * half_atoms, transcendentals=0,
            ),
            name="mix",
        )(index, half[None], *pieces, vt, gt, kt, qt, *phases, gain, *after)

    made = []
    first = 0
    phases = []
    for groups in CHUNKS:
        after = [made[-2][2]] if len(made) > 1 else []
        kept, sent, phases = make_states(first, groups, after, phases)
        made.append((kept, *crossing(kept, sent)))
        first += groups
    pieces = [piece for each in made for piece in summed(*each)]
    sent_direct = mix(1 - mine, pieces, phases, True, False)
    sent_back = mix(1 - mine, pieces, phases, False, True, [sent_direct])
    theirs_direct, theirs_back = (
        lax.ppermute(x, "dirs", [(0, 1), (1, 0)]) for x in (sent_direct, sent_back)
    )
    ours = mix(mine, pieces, phases, True, True, [sent_back])
    theirs = (
        theirs_direct[:, :feats], theirs_back[:, :feats], theirs_back[:, feats:],
        theirs_direct[:, feats:],
    )
    return tuple(
        added(ours[:, at * feats : (at + 1) * feats], other) for at, other in enumerate(theirs)
    )


def solution(mesh):
    return jax.shard_map(
        functools.partial(per_device, mesh.shape["atoms"]),
        mesh=mesh,
        in_specs=(
            P("atoms", None),
            P("atoms", None),
            P("atoms", None),
            P("atoms", None),
            P(None, "atoms"),
            P("atoms"),
            P("atoms"),
            P(),
            P(),
            P(None, "dirs"),
            P("dirs"),
            P("dirs"),
        ),
        out_specs=(
            P(("atoms", "dirs"), None),
            P(("atoms", "dirs"), None),
            P(("atoms", "dirs"), None),
            P(("atoms", "dirs"), None),
        ),
        check_vma=False,
    )
```

```python
import functools
import math

import jax
import jax.numpy as jnp
from jax import lax
from jax.experimental import pallas as pl
from jax.experimental.pallas import tpu as pltpu
from jax.sharding import PartitionSpec as P

BF16 = jnp.bfloat16
F32 = jnp.float32
GROUP = 4
QUADS = 4
LANES = 128
QUARTER = LANES // QUADS
WIDTH = GROUP * LANES
VMEM_LIMIT = 56 * 2**20
CHUNKS = (4, 4, 3)

SIN_COEF = (4.4428679, -7.30744342, 3.59478808, -0.78437403)
COS_COEF = (1.41420408, -6.97764206, 5.71523839, -1.72834866)


def cos_sin_turns(turns):
    part = turns - jnp.round(turns)
    square = part * part
    sine = SIN_COEF[2] + square * SIN_COEF[3]
    sine = SIN_COEF[1] + square * sine
    sine = part * (SIN_COEF[0] + square * sine)
    cosine = COS_COEF[2] + square * COS_COEF[3]
    cosine = COS_COEF[1] + square * cosine
    cosine = COS_COEF[0] + square * cosine
    return 1.0 - sine * sine, sine * cosine


def column(row):
    size = row.shape[1]
    at_row = lax.broadcasted_iota(jnp.int32, (size, size), 0)
    at_lane = lax.broadcasted_iota(jnp.int32, (size, size), 1)
    return jnp.sum(jnp.where(at_row == at_lane, row, 0.0), axis=1, keepdims=True)


def place_of(index):
    return index & 1, (index >> 1) & 1, (index >> 2) & 3


def slot_of(block, quad):
    away = block ^ quad
    return ((away & 1) << 1) | (away >> 1)


def prepare_kernel(
    index_ref, domain_ref, species_ref, gain_ref, q_ref, k_ref, v_ref, g_ref,
    qt_ref, kt_ref, vt_ref, gt_ref, gain_out,
):
    alive = (domain_ref[...] == index_ref[0]).astype(F32)
    species = species_ref[...]
    gain = jnp.zeros(gain_out.shape, F32)
    for s in range(gain_ref.shape[0]):
        gain = jnp.where(species == s, column(gain_ref[s : s + 1, :]), gain)
    gain_out[...] = gain
    kt_ref[...] = (k_ref[...].astype(F32).T * gain * alive).astype(BF16)
    qt_ref[...] = (q_ref[...].astype(F32).T * alive).astype(BF16)
    vt_ref[...] = (v_ref[...].astype(F32).T * alive).astype(BF16)
    gt_ref[...] = (g_ref[...].astype(F32).T * alive).astype(BF16)


def states_kernel(
    first, part, scale, index_ref, dirs_ref, weight_ref, mask_ref, freq_ref, pos_ref,
    qt_ref, kt_ref, v_ref, g_ref, *refs,
):
    kept_ref, sent_ref, cos_ref, sin_ref, kr, qr, slots = refs[-7:]
    group = first + pl.program_id(0)
    core, pair, quad = place_of(index_ref[0])
    freq = column(freq_ref[...]) * (1.0 / (2.0 * math.pi))
    for start in range(0, pos_ref.shape[1], part):
        cols = slice(start, start + part)
        cosines, sines = [], []
        for i in range(GROUP):
            u = group * GROUP + i
            proj = (
                dirs_ref[0, u] * pos_ref[0:1, cols]
                + dirs_ref[1, u] * pos_ref[1:2, cols]
                + dirs_ref[2, u] * pos_ref[2:3, cols]
            )
            cosine, sine = cos_sin_turns(freq * proj)
            cosines.append(cosine.astype(BF16))
            sines.append(sine.astype(BF16))
        cosine = jnp.concatenate(cosines, axis=0)
        sine = jnp.concatenate(sines, axis=0)
        cos_ref[:, cols] = cosine
        sin_ref[:, cols] = sine
        kr[:, cols] = rotated(kt_ref[:, cols], cosine, sine)
        qr[:, cols] = rotated(qt_ref[:, cols], cosine, sine)

    for kind, rot, other in ((0, kr, v_ref), (1, qr, g_ref)):
        total = jnp.dot(rot[...], other[...], preferred_element_type=F32)
        for i in range(GROUP):
            u = group * GROUP + i
            coef = weight_ref[u] * mask_ref[u].astype(F32) * scale
            rows = slice(i % 2 * QUARTER, (i % 2 + 1) * QUARTER)
            for m in range(QUADS):
                row = i * LANES + m * QUARTER
                slots[kind ^ core, (i // 2) ^ pair, slot_of(m, quad), rows, :] = (
                    total[row : row + QUARTER, :] * coef
                ).astype(BF16)
    kept_ref[...] = slots[0]
    sent_ref[...] = slots[1]


def rotated(x, cosine, sine):
    pieces = []
    for i in range(GROUP):
        c = cosine[i * QUARTER : (i + 1) * QUARTER]
        s = sine[i * QUARTER : (i + 1) * QUARTER]
        quarters = [x[m * QUARTER : (m + 1) * QUARTER] for m in range(QUADS)]
        pieces += [quarters[m] * c - quarters[m + 2] * s for m in range(2)]
        pieces += [quarters[m] * s + quarters[m + 2] * c for m in range(2)]
    return jnp.concatenate(pieces, axis=0)


def mix_kernel(chunks, part, index_ref, half_ref, *refs):
    del half_ref
    sources, refs = refs[: 4 * len(chunks)], refs[4 * len(chunks) :]
    vt_ref, gt_ref, kt_ref, qt_ref, cos_ref, sin_ref, gain_ref, out_ref = refs[:8]
    slots, states, states_t, *totals = refs[8:]
    group = pl.program_id(0)
    core, pair, quad = place_of(index_ref[0])

    @pl.when(group == 0)
    def _():
        done = 0
        for at, groups in enumerate(chunks):
            rows = groups * 2 * QUARTER
            for place, source in enumerate(sources[4 * at : 4 * at + 4]):
                for slot in range(QUADS):
                    slots[place // 2, place % 2, slot, done : done + rows, :] = source[
                        slot * rows : (slot + 1) * rows, :
                    ]
            done += rows
        for total in totals:
            total[...] = jnp.zeros_like(total)

    for kind in range(2):
        for i in range(GROUP):
            rows = pl.ds(
                pl.multiple_of(group * 2 * QUARTER + i % 2 * QUARTER, QUARTER), QUARTER
            )
            whole = jnp.concatenate(
                [
                    slots[kind ^ core, (i // 2) ^ pair, slot_of(m, quad), rows, :]
                    for m in range(QUADS)
                ],
                axis=0,
            )
            states[kind, i * LANES : (i + 1) * LANES, :] = whole
            states_t[kind, :, i * LANES : (i + 1) * LANES] = whole.astype(F32).T.astype(BF16)

    starts = list(range(0, vt_ref.shape[1], part))

    def backs(start):
        cols = slice(start, start + part)
        return [
            jnp.dot(states[kind], fixed[:, cols], preferred_element_type=F32)
            for kind, fixed in ((0, gt_ref), (1, vt_ref))
        ]

    def turn(start):
        cols = slice(start, start + part)
        return [
            rotated(x_ref[:, cols], cos_ref[:, cols], sin_ref[:, cols]) for x_ref in (qt_ref, kt_ref)
        ]

    back, turned = backs(starts[0]), turn(starts[0])
    for at, start in enumerate(starts):
        cols = slice(start, start + part)
        for kind, direct in ((0, totals[0]), (1, totals[3])):
            direct[:, cols] += jnp.dot(
                states_t[kind], turned[kind], preferred_element_type=F32
            )
        if start != starts[-1]:
            next_back = backs(starts[at + 1])
        cosine = cos_ref[:, cols]
        sine = sin_ref[:, cols]
        for kind, total in ((0, totals[1]), (1, totals[2])):
            lower = back[kind].astype(BF16)
            for m in range(2):
                leads, trails = [], []
                for i in range(GROUP):
                    c = cosine[i * QUARTER : (i + 1) * QUARTER]
                    s = sine[i * QUARTER : (i + 1) * QUARTER]
                    row = i * LANES + QUARTER * m
                    lead = lower[row : row + QUARTER, :]
                    trail = lower[row + 2 * QUARTER : row + 3 * QUARTER, :]
                    leads.append(lead * c + trail * s)
                    trails.append(trail * c - lead * s)
                for block, terms in ((m, leads), (m + 2, trails)):
                    rows = slice(QUARTER * block, QUARTER * (block + 1))
                    total[rows, cols] += ((terms[0] + terms[1]) + (terms[2] + terms[3])).astype(F32)
        if start != starts[-1]:
            back, turned = next_back, turn(starts[at + 1])

    @pl.when(group == pl.num_programs(0) - 1)
    def _():
        for at, total in enumerate(totals):
            whole = total[...] * gain_ref[...] if at == 2 else total[...]
            out_ref[:, at * LANES : (at + 1) * LANES] = whole.T.astype(out_ref.dtype)


def added(*terms):
    return sum(term.astype(F32) for term in terms).astype(BF16)


def per_device(
    atom_devices, queries, keys, values, cotangent, positions, species, domain, species_gain,
    frequency, directions, dir_weight, dir_mask,
):
    atoms, feats = queries.shape
    total_groups = dir_weight.shape[0] // GROUP
    half_atoms = atoms // 2
    index = lax.axis_index("atoms")[None].astype(jnp.int32)
    mine = lax.axis_index("dirs").astype(jnp.int32)
    vmem = pl.BlockSpec(memory_space=pltpu.VMEM)
    smem = pl.BlockSpec(memory_space=pltpu.SMEM)
    anywhere = pl.BlockSpec(memory_space=pl.ANY)
    params = pltpu.CompilerParams(vmem_limit_bytes=VMEM_LIMIT)
    shape = jax.ShapeDtypeStruct

    qt, kt, vt, gt, gain = pl.pallas_call(
        prepare_kernel,
        in_specs=[smem] + [vmem] * 7,
        out_specs=[vmem] * 5,
        out_shape=[shape((feats, atoms), BF16)] * 4 + [shape((feats, atoms), F32)],
        compiler_params=params,
        name="prepare",
    )(index, domain[None, :], species[None, :], species_gain, queries, keys, values, cotangent)

    def make_states(first, groups, after, phases):
        sent = shape((2, QUADS, groups * 2 * QUARTER, feats), BF16)
        sent_spec = pl.BlockSpec((2, QUADS, 2 * QUARTER, feats), lambda g: (0, 0, g, 0))
        phase = shape((total_groups * GROUP * QUARTER, atoms), BF16)
        phase_spec = pl.BlockSpec((GROUP * QUARTER, atoms), lambda g: (g + first, 0))
        operands = [
            index, directions, dir_weight, dir_mask, frequency[None, :], positions, qt, kt,
            values, cotangent, *after,
        ]
        kept, sent, *phases = pl.pallas_call(
            functools.partial(states_kernel, first, min(256, atoms), 1.0 / math.sqrt(feats * atoms)),
            grid=(groups,),
            in_specs=[smem] * 4 + [vmem] * 6 + [anywhere] * (len(after) + len(phases)),
            out_specs=[sent_spec] * 2 + [phase_spec] * 2,
            out_shape=[sent] * 2 + [phase] * 2,
            input_output_aliases={len(operands) + at: 2 + at for at in range(len(phases))},
            scratch_shapes=[pltpu.VMEM((WIDTH, atoms), BF16)] * 2
            + [pltpu.VMEM((2, 2, QUADS, 2 * QUARTER, feats), BF16)],
            compiler_params=params,
            cost_estimate=pl.CostEstimate(
                flops=8 * groups * WIDTH * atoms * feats,
                bytes_accessed=2 * groups * WIDTH * atoms, transcendentals=0,
            ),
            name="states",
        )(*operands, *phases)
        return kept, sent, phases

    def moved(x, target):
        return lax.ppermute(x, "atoms", [(i, target(i)) for i in range(atom_devices)])

    def by_bit(x, bit):
        return moved(x, lambda i: i ^ bit)

    def crossing(kept, sent):
        arrived = by_bit(sent, 1)
        return arrived, added(kept[1], arrived[1])

    def summed(kept, arrived, crossing_out):
        half = added(kept[0], arrived[0], by_bit(crossing_out, 2))
        near = added(half[:2], by_bit(half[2:], 4))
        near = added(near, by_bit(near, 8)[::-1])
        total = near
        for step in range(16, atom_devices, 16):
            total = added(total, moved(near, lambda i: (i + step) % atom_devices))
        near = total.reshape(-1, feats)
        half = jnp.concatenate([near, by_bit(near, 4)], axis=0)
        other = by_bit(half, 2)
        return half, other, by_bit(half, 1), by_bit(other, 1)

    def mix(half, pieces, phases, dtype, after=()):
        rows_half = pl.BlockSpec((feats, half_atoms), lambda g, index, half: (0, half[0]))
        phase_spec = pl.BlockSpec(
            (GROUP * QUARTER, half_atoms), lambda g, index, half: (g, half[0])
        )
        return pl.pallas_call(
            lambda *refs: mix_kernel(
                CHUNKS, min(256, half_atoms), *refs[: 2 + len(pieces) + 7],
                *refs[2 + len(pieces) + 7 + len(after) :],
            ),
            grid_spec=pltpu.PrefetchScalarGridSpec(
                num_scalar_prefetch=2,
                grid=(total_groups,),
                in_specs=[vmem] * len(pieces) + [rows_half] * 4 + [phase_spec] * 2 + [rows_half]
                + [anywhere] * len(after),
                out_specs=pl.BlockSpec((half_atoms, 4 * feats), lambda g, index, half: (0, 0)),
                scratch_shapes=[
                    pltpu.VMEM((2, 2, QUADS, total_groups * 2 * QUARTER, feats), BF16),
                    pltpu.VMEM((2, WIDTH, feats), BF16),
                    pltpu.VMEM((2, feats, WIDTH), BF16),
                ]
                + [pltpu.VMEM((feats, half_atoms), F32)] * 4,
            ),
            out_shape=shape((half_atoms, 4 * feats), dtype),
            compiler_params=params,
            cost_estimate=pl.CostEstimate(
                flops=8 * total_groups * WIDTH * half_atoms * feats,
                bytes_accessed=2 * total_groups * WIDTH * half_atoms, transcendentals=0,
            ),
            name="mix",
        )(index, half[None], *pieces, vt, gt, kt, qt, *phases, gain, *after)

    made = []
    first = 0
    phases = []
    for groups in CHUNKS:
        after = [made[-2][2]] if len(made) > 1 else []
        kept, sent, phases = make_states(first, groups, after, phases)
        made.append((kept, *crossing(kept, sent)))
        first += groups
    pieces = [piece for each in made for piece in summed(*each)]
    sent = mix(1 - mine, pieces, phases, BF16)
    theirs = lax.ppermute(sent, "dirs", [(0, 1), (1, 0)])
    ours = mix(mine, pieces, phases, F32, [sent])
    lanes = [slice(at * feats, (at + 1) * feats) for at in range(4)]
    return tuple((ours[:, at] + theirs[:, at].astype(F32)).astype(BF16) for at in lanes)


def solution(mesh):
    return jax.shard_map(
        functools.partial(per_device, mesh.shape["atoms"]),
        mesh=mesh,
        in_specs=(
            P("atoms", None),
            P("atoms", None),
            P("atoms", None),
            P("atoms", None),
            P(None, "atoms"),
            P("atoms"),
            P("atoms"),
            P(),
            P(),
            P(None, "dirs"),
            P("dirs"),
            P("dirs"),
        ),
        out_specs=(
            P(("atoms", "dirs"), None),
            P(("atoms", "dirs"), None),
            P(("atoms", "dirs"), None),
            P(("atoms", "dirs"), None),
        ),
        check_vma=False,
    )
```

```python
import functools
import math

import jax
import jax.numpy as jnp
from jax import lax
from jax.experimental import pallas as pl
from jax.experimental.pallas import tpu as pltpu
from jax.sharding import PartitionSpec as P

BF16 = jnp.bfloat16
F32 = jnp.float32
GROUP = 4
QUADS = 4
LANES = 128
QUARTER = LANES // QUADS
WIDTH = GROUP * LANES
VMEM_LIMIT = 56 * 2**20
CHUNKS = (4, 4, 3)

SIN_COEF = (4.4428679, -7.30744342, 3.59478808, -0.78437403)
COS_COEF = (1.41420408, -6.97764206, 5.71523839, -1.72834866)


def cos_sin_turns(turns):
    part = turns - jnp.round(turns)
    square = part * part
    sine = SIN_COEF[2] + square * SIN_COEF[3]
    sine = SIN_COEF[1] + square * sine
    sine = part * (SIN_COEF[0] + square * sine)
    cosine = COS_COEF[2] + square * COS_COEF[3]
    cosine = COS_COEF[1] + square * cosine
    cosine = COS_COEF[0] + square * cosine
    return 1.0 - sine * sine, sine * cosine


def column(row):
    size = row.shape[1]
    at_row = lax.broadcasted_iota(jnp.int32, (size, size), 0)
    at_lane = lax.broadcasted_iota(jnp.int32, (size, size), 1)
    return jnp.sum(jnp.where(at_row == at_lane, row, 0.0), axis=1, keepdims=True)


def place_of(index):
    return index & 1, (index >> 1) & 1, (index >> 2) & 3


def slot_of(block, quad):
    away = block ^ quad
    return ((away & 1) << 1) | (away >> 1)


def prepare_kernel(
    index_ref, domain_ref, species_ref, gain_ref, q_ref, k_ref, v_ref, g_ref,
    qt_ref, kt_ref, vt_ref, gt_ref, gain_out,
):
    alive = (domain_ref[...] == index_ref[0]).astype(F32)
    species = species_ref[...]
    gain = jnp.zeros(gain_out.shape, F32)
    for s in range(gain_ref.shape[0]):
        gain = jnp.where(species == s, column(gain_ref[s : s + 1, :]), gain)
    gain_out[...] = gain
    kt_ref[...] = (k_ref[...].astype(F32).T * gain * alive).astype(BF16)
    qt_ref[...] = (q_ref[...].astype(F32).T * alive).astype(BF16)
    vt_ref[...] = (v_ref[...].astype(F32).T * alive).astype(BF16)
    gt_ref[...] = (g_ref[...].astype(F32).T * alive).astype(BF16)


def states_kernel(
    first, part, scale, index_ref, dirs_ref, weight_ref, mask_ref, freq_ref, pos_ref,
    qt_ref, kt_ref, v_ref, g_ref, *refs,
):
    kept_ref, sent_ref, cos_ref, sin_ref, kr, qr, slots = refs[-7:]
    group = first + pl.program_id(0)
    core, pair, quad = place_of(index_ref[0])
    freq = column(freq_ref[...]) * (1.0 / (2.0 * math.pi))
    for start in range(0, pos_ref.shape[1], part):
        cols = slice(start, start + part)
        cosines, sines = [], []
        for i in range(GROUP):
            u = group * GROUP + i
            proj = (
                dirs_ref[0, u] * pos_ref[0:1, cols]
                + dirs_ref[1, u] * pos_ref[1:2, cols]
                + dirs_ref[2, u] * pos_ref[2:3, cols]
            )
            cosine, sine = cos_sin_turns(freq * proj)
            cosines.append(cosine.astype(BF16))
            sines.append(sine.astype(BF16))
        cosine = jnp.concatenate(cosines, axis=0)
        sine = jnp.concatenate(sines, axis=0)
        cos_ref[:, cols] = cosine
        sin_ref[:, cols] = sine
        kr[:, cols] = rotated(kt_ref[:, cols], cosine, sine)
        qr[:, cols] = rotated(qt_ref[:, cols], cosine, sine)

    for kind, rot, other in ((0, kr, v_ref), (1, qr, g_ref)):
        total = jnp.dot(rot[...], other[...], preferred_element_type=F32)
        for i in range(GROUP):
            u = group * GROUP + i
            coef = weight_ref[u] * mask_ref[u].astype(F32) * scale
            rows = slice(i % 2 * QUARTER, (i % 2 + 1) * QUARTER)
            for m in range(QUADS):
                row = i * LANES + m * QUARTER
                slots[kind ^ core, (i // 2) ^ pair, slot_of(m, quad), rows, :] = (
                    total[row : row + QUARTER, :] * coef
                ).astype(BF16)
    kept_ref[...] = slots[0]
    sent_ref[...] = slots[1]


def rotated(x, cosine, sine):
    pieces = []
    for i in range(GROUP):
        c = cosine[i * QUARTER : (i + 1) * QUARTER]
        s = sine[i * QUARTER : (i + 1) * QUARTER]
        quarters = [x[m * QUARTER : (m + 1) * QUARTER] for m in range(QUADS)]
        pieces += [quarters[m] * c - quarters[m + 2] * s for m in range(2)]
        pieces += [quarters[m] * s + quarters[m + 2] * c for m in range(2)]
    return jnp.concatenate(pieces, axis=0)


def mix_kernel(chunks, part, index_ref, half_ref, *refs):
    del half_ref
    sources, refs = refs[: 4 * len(chunks)], refs[4 * len(chunks) :]
    vt_ref, gt_ref, kt_ref, qt_ref, cos_ref, sin_ref, gain_ref, out_ref = refs[:8]
    slots, states, states_t, *totals = refs[8:]
    group = pl.program_id(0)
    core, pair, quad = place_of(index_ref[0])

    @pl.when(group == 0)
    def _():
        done = 0
        for at, groups in enumerate(chunks):
            rows = groups * 2 * QUARTER
            for place, source in enumerate(sources[4 * at : 4 * at + 4]):
                for slot in range(QUADS):
                    slots[place // 2, place % 2, slot, done : done + rows, :] = source[
                        slot * rows : (slot + 1) * rows, :
                    ]
            done += rows
        for total in totals:
            total[...] = jnp.zeros_like(total)

    for kind in range(2):
        for i in range(GROUP):
            rows = pl.ds(
                pl.multiple_of(group * 2 * QUARTER + i % 2 * QUARTER, QUARTER), QUARTER
            )
            whole = jnp.concatenate(
                [
                    slots[kind ^ core, (i // 2) ^ pair, slot_of(m, quad), rows, :]
                    for m in range(QUADS)
                ],
                axis=0,
            )
            states[kind, i * LANES : (i + 1) * LANES, :] = whole
            states_t[kind, :, i * LANES : (i + 1) * LANES] = whole.astype(F32).T.astype(BF16)

    starts = list(range(0, vt_ref.shape[1], part))

    def backs(start):
        cols = slice(start, start + part)
        return [
            jnp.dot(states[kind], fixed[:, cols], preferred_element_type=F32)
            for kind, fixed in ((0, gt_ref), (1, vt_ref))
        ]

    def turn(start):
        cols = slice(start, start + part)
        return [
            rotated(x_ref[:, cols], cos_ref[:, cols], sin_ref[:, cols]) for x_ref in (qt_ref, kt_ref)
        ]

    back, turned = backs(starts[0]), turn(starts[0])
    for at, start in enumerate(starts):
        cols = slice(start, start + part)
        for kind, direct in ((0, totals[0]), (1, totals[3])):
            direct[:, cols] += jnp.dot(
                states_t[kind], turned[kind], preferred_element_type=F32
            )
        if start != starts[-1]:
            next_back = backs(starts[at + 1])
        cosine = cos_ref[:, cols]
        sine = sin_ref[:, cols]
        for kind, total in ((0, totals[1]), (1, totals[2])):
            lower = back[kind].astype(BF16)
            for m in range(2):
                leads, trails = [], []
                for i in range(GROUP):
                    c = cosine[i * QUARTER : (i + 1) * QUARTER]
                    s = sine[i * QUARTER : (i + 1) * QUARTER]
                    row = i * LANES + QUARTER * m
                    lead = lower[row : row + QUARTER, :]
                    trail = lower[row + 2 * QUARTER : row + 3 * QUARTER, :]
                    leads.append(lead * c + trail * s)
                    trails.append(trail * c - lead * s)
                for block, terms in ((m, leads), (m + 2, trails)):
                    rows = slice(QUARTER * block, QUARTER * (block + 1))
                    total[rows, cols] += ((terms[0] + terms[1]) + (terms[2] + terms[3])).astype(F32)
        if start != starts[-1]:
            back, turned = next_back, turn(starts[at + 1])

    @pl.when(group == pl.num_programs(0) - 1)
    def _():
        for at, total in enumerate(totals):
            whole = total[...] * gain_ref[...] if at == 2 else total[...]
            out_ref[:, at * LANES : (at + 1) * LANES] = whole.T.astype(out_ref.dtype)


def added(*terms):
    return sum(term.astype(F32) for term in terms).astype(BF16)


def per_device(
    atom_devices, queries, keys, values, cotangent, positions, species, domain, species_gain,
    frequency, directions, dir_weight, dir_mask,
):
    atoms, feats = queries.shape
    total_groups = dir_weight.shape[0] // GROUP
    half_atoms = atoms // 2
    index = lax.axis_index("atoms")[None].astype(jnp.int32)
    mine = lax.axis_index("dirs").astype(jnp.int32)
    vmem = pl.BlockSpec(memory_space=pltpu.VMEM)
    smem = pl.BlockSpec(memory_space=pltpu.SMEM)
    anywhere = pl.BlockSpec(memory_space=pl.ANY)
    params = pltpu.CompilerParams(vmem_limit_bytes=VMEM_LIMIT)
    shape = jax.ShapeDtypeStruct

    qt, kt, vt, gt, gain = pl.pallas_call(
        prepare_kernel,
        in_specs=[smem] + [vmem] * 7,
        out_specs=[vmem] * 5,
        out_shape=[shape((feats, atoms), BF16)] * 4 + [shape((feats, atoms), F32)],
        compiler_params=params,
        name="prepare",
    )(index, domain[None, :], species[None, :], species_gain, queries, keys, values, cotangent)

    def make_states(first, groups, after, phases):
        sent = shape((2, QUADS, groups * 2 * QUARTER, feats), BF16)
        sent_spec = pl.BlockSpec((2, QUADS, 2 * QUARTER, feats), lambda g: (0, 0, g, 0))
        phase = shape((total_groups * GROUP * QUARTER, atoms), BF16)
        phase_spec = pl.BlockSpec((GROUP * QUARTER, atoms), lambda g: (g + first, 0))
        operands = [
            index, directions, dir_weight, dir_mask, frequency[None, :], positions, qt, kt,
            values, cotangent, *after,
        ]
        kept, sent, *phases = pl.pallas_call(
            functools.partial(states_kernel, first, min(256, atoms), 1.0 / math.sqrt(feats * atoms)),
            grid=(groups,),
            in_specs=[smem] * 4 + [vmem] * 6 + [anywhere] * (len(after) + len(phases)),
            out_specs=[sent_spec] * 2 + [phase_spec] * 2,
            out_shape=[sent] * 2 + [phase] * 2,
            input_output_aliases={len(operands) + at: 2 + at for at in range(len(phases))},
            scratch_shapes=[pltpu.VMEM((WIDTH, atoms), BF16)] * 2
            + [pltpu.VMEM((2, 2, QUADS, 2 * QUARTER, feats), BF16)],
            compiler_params=params,
            cost_estimate=pl.CostEstimate(
                flops=8 * groups * WIDTH * atoms * feats,
                bytes_accessed=2 * groups * WIDTH * atoms, transcendentals=0,
            ),
            name="states",
        )(*operands, *phases)
        return kept, sent, phases

    def moved(x, target):
        return lax.ppermute(x, "atoms", [(i, target(i)) for i in range(atom_devices)])

    def by_bit(x, bit):
        return moved(x, lambda i: i ^ bit)

    def crossing(kept, sent):
        arrived = by_bit(sent, 1)
        return arrived, added(kept[1], arrived[1])

    def summed(kept, arrived, crossing_out):
        half = added(kept[0], arrived[0], by_bit(crossing_out, 2))
        near = added(half[:2], by_bit(half[2:], 4))
        near = added(near, by_bit(near, 8)[::-1])
        total = near
        for step in range(16, atom_devices, 16):
            total = added(total, moved(near, lambda i: (i + step) % atom_devices))
        near = total.reshape(-1, feats)
        half = jnp.concatenate([near, by_bit(near, 4)], axis=0)
        other = by_bit(half, 2)
        return half, other, by_bit(half, 1), by_bit(other, 1)

    def mix(half, pieces, phases, dtype, after=()):
        rows_half = pl.BlockSpec((feats, half_atoms), lambda g, index, half: (0, half[0]))
        phase_spec = pl.BlockSpec(
            (GROUP * QUARTER, half_atoms), lambda g, index, half: (g, half[0])
        )
        return pl.pallas_call(
            lambda *refs: mix_kernel(
                CHUNKS, min(512, half_atoms), *refs[: 2 + len(pieces) + 7],
                *refs[2 + len(pieces) + 7 + len(after) :],
            ),
            grid_spec=pltpu.PrefetchScalarGridSpec(
                num_scalar_prefetch=2,
                grid=(total_groups,),
                in_specs=[vmem] * len(pieces) + [rows_half] * 4 + [phase_spec] * 2 + [rows_half]
                + [anywhere] * len(after),
                out_specs=pl.BlockSpec((half_atoms, 4 * feats), lambda g, index, half: (0, 0)),
                scratch_shapes=[
                    pltpu.VMEM((2, 2, QUADS, total_groups * 2 * QUARTER, feats), BF16),
                    pltpu.VMEM((2, WIDTH, feats), BF16),
                    pltpu.VMEM((2, feats, WIDTH), BF16),
                ]
                + [pltpu.VMEM((feats, half_atoms), F32)] * 4,
            ),
            out_shape=shape((half_atoms, 4 * feats), dtype),
            compiler_params=params,
            cost_estimate=pl.CostEstimate(
                flops=8 * total_groups * WIDTH * half_atoms * feats,
                bytes_accessed=2 * total_groups * WIDTH * half_atoms, transcendentals=0,
            ),
            name="mix",
        )(index, half[None], *pieces, vt, gt, kt, qt, *phases, gain, *after)

    made = []
    first = 0
    phases = []
    for groups in CHUNKS:
        after = [made[-2][2]] if len(made) > 1 else []
        kept, sent, phases = make_states(first, groups, after, phases)
        made.append((kept, *crossing(kept, sent)))
        first += groups
    pieces = [piece for each in made for piece in summed(*each)]
    sent = mix(1 - mine, pieces, phases, BF16)
    theirs = lax.ppermute(sent, "dirs", [(0, 1), (1, 0)])
    ours = mix(mine, pieces, phases, BF16, [sent])
    lanes = [slice(at * feats, (at + 1) * feats) for at in range(4)]
    return tuple((ours[:, at] + theirs[:, at].astype(F32)).astype(BF16) for at in lanes)


def solution(mesh):
    return jax.shard_map(
        functools.partial(per_device, mesh.shape["atoms"]),
        mesh=mesh,
        in_specs=(
            P("atoms", None),
            P("atoms", None),
            P("atoms", None),
            P("atoms", None),
            P(None, "atoms"),
            P("atoms"),
            P("atoms"),
            P(),
            P(),
            P(None, "dirs"),
            P("dirs"),
            P("dirs"),
        ),
        out_specs=(
            P(("atoms", "dirs"), None),
            P(("atoms", "dirs"), None),
            P(("atoms", "dirs"), None),
            P(("atoms", "dirs"), None),
        ),
        check_vma=False,
    )
```
